512 devices in a mesh: row: 64 (over z_hi, y, core), key: 8 (over z_lo, x).
Axes of the slice: x: 4, y: 8, z: 8 (z_hi: 4, z_lo: 2; z = z_hi * 2 + z_lo), core: 2. Of those that a mesh axis runs over, the one named last changes fastest.
Arguments:
- queries: bfloat16 [256, 1024, 128], P('row', 'key'), may hold values from -28 to 28
- keys_in: bfloat16 [256, 1024, 128], P('row', 'key'), may hold values from -28 to 28
- values: bfloat16 [256, 1024, 128], P('row', 'key'), may hold values from -6 to 6
- cotangent: bfloat16 [256, 1024, 128], P('row', 'key'), may hold values from -48 to 48
- pair_bias: bfloat16 [4, 1024, 1024], P(None, ('key', 'row')), may hold values from -6 to 6
- key_lengths: int32 [256], P('row'), may hold values from 256 to 1024
Outputs:
- grad_queries: bfloat16 [256, 1024, 128], P('row', 'key')
- grad_keys: bfloat16 [256, 1024, 128], P('row', 'key')
- grad_values: bfloat16 [256, 1024, 128], P('row', 'key')
- grad_bias: float32 [4, 1024, 1024], P(None, ('key', 'row'))
The draws below stay inside these ranges and needn't reach their ends.
All inputs are finite; a program needn't handle non-finite values.
Results may differ from the reference program's by a relative error of at most 0.035.
Values may be sent and summed in bfloat16 or wider, within the bound.
A program may use at most 64 MiB of HBM per device.

```python
import math
import jax
import jax.numpy as jnp
from jax import lax

HEADS = 4
HEAD_DIM = 32
CROP = 1024
PAIR_DIM = 128
PAIR_ROWS = 256
N_KEY = 8


def draw_queries(key, part):
    key = jax.random.fold_in(key, 11)
    drawn = jax.random.truncated_normal(key, -4.0, 4.0, (PAIR_ROWS, CROP, HEADS * HEAD_DIM), jnp.float32)
    return drawn.astype(jnp.bfloat16)


def draw_keys_in(key, part):
    key = jax.random.fold_in(key, 23)
    drawn = jax.random.truncated_normal(key, -4.0, 4.0, (PAIR_ROWS, CROP, HEADS * HEAD_DIM), jnp.float32)
    return drawn.astype(jnp.bfloat16)


def with_ends(values, rng, smallest, high):
    longest = values.shape.index(max(values.shape))
    spots = []
    for shift in (0, 1):
        where = [jax.random.randint(jax.random.fold_in(rng, axis), (), 0, length) for axis, length in enumerate(values.shape)]
        where[longest] = (where[longest] + shift) % values.shape[longest]
        spots.append(tuple(where))
    return values.at[spots[0]].set(smallest).at[spots[1]].set(high)


def steps_of(key, extent, pieces, least, high):
    factor_of, own = 1.0, jax.random.fold_in(key, 6)
    for dim, parts in pieces:
        draws = jnp.exp(jax.random.uniform(jax.random.fold_in(own, dim), (parts,), jnp.float32, least / len(pieces), high / len(pieces)))
        factor_of = factor_of * jnp.repeat(draws, extent[dim] // parts).reshape([-1 if axis == dim else 1 for axis in range(len(extent))])
    return factor_of


def normal_values(stream_key, shape, spread, bound, shards=(), kind=jnp.bfloat16):
    values = jax.random.normal(stream_key, shape, jnp.float32) * spread
    if len(shards) > 0:
        values = steps_of(stream_key, shape, shards, -0.22, 0.18) * values
    return jnp.clip(values, min=-bound, max=bound).astype(kind)


def setup_inputs(seed: int = 0) -> dict:
    key_of = jax.random.split(jax.random.key(seed), 7)
    queries = draw_queries(jax.random.fold_in(key_of[6], 71), 0)
    keys_in = draw_keys_in(jax.random.fold_in(key_of[6], 71), 0)
    values = normal_values(key_of[2], (PAIR_ROWS, CROP, PAIR_DIM), 1.0, 6.0, ((0, 64), (1, 8)))
    cotangent = normal_values(key_of[3], (PAIR_ROWS, CROP, PAIR_DIM), 8.0, 48.0, ((0, 64), (1, 8)))
    pair_bias = normal_values(key_of[4], (HEADS, CROP, CROP), 1.0, 6.0, ((1, 512),))
    key_lengths = with_ends(jax.random.randint(key_of[5], (PAIR_ROWS,), CROP // 4, CROP + 1), jax.random.fold_in(key_of[5], 1), CROP // 4, CROP).astype(jnp.int32)
    return dict(queries=queries, keys_in=keys_in, values=values, cotangent=cotangent, pair_bias=pair_bias, key_lengths=key_lengths)


def row_terms(query_row, key_row, value_row, grad_row, length, bias_float):
    factor = 1.0 / math.sqrt(HEAD_DIM)
    query_heads = query_row.astype(jnp.float32).reshape(CROP, HEADS, HEAD_DIM)
    key_heads = key_row.astype(jnp.float32).reshape(CROP, HEADS, HEAD_DIM)
    value_heads = value_row.astype(jnp.float32).reshape(CROP, HEADS, HEAD_DIM)
    grad_heads = grad_row.astype(jnp.float32).reshape(CROP, HEADS, HEAD_DIM)
    scores = jnp.einsum('jhd,khd->hjk', query_heads, key_heads) * factor + bias_float
    key_pos = jnp.arange(CROP, dtype=jnp.int32)
    scores = jnp.where((key_pos < length)[None, None, :], scores, -1e+30)
    row_max = lax.optimization_barrier(jnp.max(scores, axis=-1, keepdims=True))
    log_total = row_max + jnp.log(lax.optimization_barrier(jnp.sum(jnp.exp(scores - row_max), axis=-1, keepdims=True)))
    weights = jnp.exp(scores - log_total)
    weights_low = weights.astype(jnp.bfloat16).astype(jnp.float32)
    attended = jnp.einsum('hjk,khd->jhd', weights_low, value_heads)
    row_dot = jnp.transpose(lax.optimization_barrier(jnp.sum(grad_heads * attended, axis=-1)), (1, 0))
    grad_weights = jnp.einsum('jhd,khd->hjk', grad_heads, value_heads)
    grad_scores = weights * (grad_weights - row_dot[:, :, None])
    grad_low = grad_scores.astype(jnp.bfloat16).astype(jnp.float32)
    grad_query = (jnp.einsum('hjk,khd->jhd', grad_low, key_heads) * factor).astype(jnp.bfloat16)
    block_len = CROP // N_KEY
    grad_blocks = grad_low.reshape(HEADS, N_KEY, block_len, CROP)
    weight_blocks = weights_low.reshape(HEADS, N_KEY, block_len, CROP)
    query_blocks = query_heads.reshape(N_KEY, block_len, HEADS, HEAD_DIM)
    cot_blocks = grad_heads.reshape(N_KEY, block_len, HEADS, HEAD_DIM)
    key_part = (jnp.einsum('hcjk,cjhd->ckhd', grad_blocks, query_blocks) * factor).astype(jnp.bfloat16)
    value_part = jnp.einsum('hcjk,cjhd->ckhd', weight_blocks, cot_blocks).astype(jnp.bfloat16)
    grad_key = lax.optimization_barrier(jnp.sum(key_part.astype(jnp.float32), axis=0)).astype(jnp.bfloat16)
    grad_value = lax.optimization_barrier(jnp.sum(value_part.astype(jnp.float32), axis=0)).astype(jnp.bfloat16)
    return (grad_query.reshape(CROP, PAIR_DIM), grad_key.reshape(CROP, PAIR_DIM), grad_value.reshape(CROP, PAIR_DIM), grad_scores)

def reference(queries, keys_in, values, cotangent, pair_bias, key_lengths):
    bias_float = pair_bias.astype(jnp.float32)

    def one_row(bias_total, inputs):
        query_row, key_row, value_row, grad_row, length = inputs
        grad_query, grad_key, grad_value, grad_scores = row_terms(query_row, key_row, value_row, grad_row, length, bias_float)
        return (bias_total + grad_scores, (grad_query, grad_key, grad_value))
    start_total = jnp.zeros((HEADS, CROP, CROP), jnp.float32)
    bias_total, results = lax.scan(one_row, start_total, (queries, keys_in, values, cotangent, key_lengths))
    return (results[0], results[1], results[2], bias_total)
```

```python
import math

import jax
import jax.numpy as jnp
from jax import lax
from jax.experimental import pallas as pl
from jax.experimental.pallas import tpu as pltpu
from jax.sharding import PartitionSpec as P

MESH = pl.DeviceIdType.MESH
VM = pltpu.VMEM
BF = jnp.bfloat16
F32 = jnp.float32
NX, NA = 4, 2
NY, NC = 8, 2
LOG2E = 1.4426950408889634


def place():
    row, key = lax.axis_index("row"), lax.axis_index("key")
    return (
        row,
        key,
        lax.div(key, NX),
        lax.rem(key, NX),
        lax.div(row, NY * NC),
        lax.rem(lax.div(row, NC), NY),
        lax.rem(row, NC),
    )


def row_of(z, y, core):
    return (z * NY + y) * NC + core


def greet(nz):
    row, key, a, x, z, y, core = place()
    barrier = pltpu.get_barrier_semaphore()
    peers = [(row, lax.rem(key + s, NA * NX)) for s in range(1, NA * NX)]
    peers += [(row_of(lax.rem(z + s, nz), y, core), key) for s in range(1, nz)]
    peers += [(row_of(z, lax.rem(y + s, NY), core), key) for s in range(1, NY)]
    peers += [(row_of(z, y, 1 - core), key)]
    for peer in peers:
        pl.semaphore_signal(barrier, inc=1, device_id=peer, device_id_type=MESH)
    pl.semaphore_wait(barrier, len(peers))


def remote(src, dst, send, recv, index, peer):
    return pltpu.make_async_remote_copy(
        src_ref=src,
        dst_ref=dst,
        send_sem=send.at[index],
        recv_sem=recv.at[index],
        device_id=peer,
        device_id_type=MESH,
    )


def gather_kernel(
    nz, q, k, v, c, bias, kv, qc, bg, own, kvs, qcs,
    s0, r0, s1a, r1a, s1b, r1b, s2a, r2a, s2b, r2b, s3, r3, skv, rkv, sqc, rqc, loc,
):
    row, key, a, x, z, y, core = place()
    rows_dev = q.shape[0]
    dim = q.shape[2] // NX
    greet(nz)
    first = []
    for s in range(1, NX):
        to = lax.rem(x + s, NX)
        cp = remote(bias.at[to], own.at[x], s0, r0, s - 1, (row, a * NX + to))
        cp.start()
        first.append(cp)
    own[x] = bias[x]
    for part, source in enumerate((k, v)):
        for i in range(rows_dev):
            turned = source[i].T
            for h in range(NX):
                kvs[h, part, i] = turned[h * dim : (h + 1) * dim]
    for cp in first:
        cp.wait()
    bg[z, y, core] = own[...]
    phase1a, phase1b = [], []
    for s in range(1, nz):
        cp = remote(
            own.at[0:2], bg.at[z, y, core, 0:2], s1a, r1a, s - 1,
            (row_of(lax.rem(z + s, nz), y, core), key),
        )
        cp.start()
        phase1a.append(cp)
    for s in range(1, NY):
        cp = remote(
            own.at[2:4], bg.at[z, y, core, 2:4], s1b, r1b, s - 1,
            (row_of(z, lax.rem(y + s, NY), core), key),
        )
        cp.start()
        phase1b.append(cp)
    others = []
    for s in range(1, NA * NX):
        to = lax.rem(key + s, NA * NX)
        cp = remote(
            kvs.at[lax.rem(to, NX)], kv.at[:, :, :, pl.ds(key * 128, 128)],
            skv, rkv, s - 1, (row, to),
        )
        cp.start()
        others.append(cp)
    for part, source in enumerate((q, c)):
        for i in range(rows_dev):
            turned = source[i].T
            for h in range(NX):
                qcs[h, part, i] = turned[h * dim : (h + 1) * dim]
    for s in range(1, NX):
        to = lax.rem(x + s, NX)
        cp = remote(
            qcs.at[to], qc.at[:, :, :, pl.ds(x * 128, 128)],
            sqc, rqc, s - 1, (row, a * NX + to),
        )
        cp.start()
        others.append(cp)
    mine = [
        pltpu.make_async_copy(kvs.at[x], kv.at[:, :, :, pl.ds(key * 128, 128)], loc.at[0]),
        pltpu.make_async_copy(qcs.at[x], qc.at[:, :, :, pl.ds(x * 128, 128)], loc.at[1]),
    ]
    for cp in mine:
        cp.start()
    for cp in phase1a:
        cp.wait()
    phase2a, phase2b = [], []
    for s in range(1, NY):
        cp = remote(
            bg.at[:, y, core, 0:2], bg.at[:, y, core, 0:2], s2a, r2a, s - 1,
            (row_of(z, lax.rem(y + s, NY), core), key),
        )
        cp.start()
        phase2a.append(cp)
    for cp in phase1b:
        cp.wait()
    for s in range(1, nz):
        cp = remote(
            bg.at[z, :, core, 2:4], bg.at[z, :, core, 2:4], s2b, r2b, s - 1,
            (row_of(lax.rem(z + s, nz), y, core), key),
        )
        cp.start()
        phase2b.append(cp)
    partner = (row_of(z, y, 1 - core), key)
    phase3 = []
    for s in range(NY):
        if s:
            phase2a[s - 1].wait()
        at = lax.rem(y + NY - s, NY)
        cp = remote(
            bg.at[:, at, core, 0:2], bg.at[:, at, core, 0:2], s3, r3, s, partner
        )
        cp.start()
        phase3.append(cp)
    for s in range(nz):
        if s:
            phase2b[s - 1].wait()
        at = lax.rem(z + nz - s, nz)
        cp = remote(
            bg.at[at, :, core, 2:4], bg.at[at, :, core, 2:4], s3, r3, NY + s, partner
        )
        cp.start()
        phase3.append(cp)
    for cp in mine + others + phase3:
        cp.wait()


def tile_kernel(nz, lengths, kv, qc, bg, dkv, gq, gb, q3, k3, cs, bias_f, total, stage, acc):
    rows_dev, dim, length = kv.shape[1:]
    mine = qc.shape[3]
    factor = 1.0 / math.sqrt(dim)
    tile = 128
    groups = NY * NC // 4

    def lay(n, carry):
        b, zz = n // nz, n % nz
        block = bg[zz, :, :, b].astype(F32) * LOG2E
        stage[...] = block.reshape(NY * NC * 16, 128)
        for g in range(groups):
            for t in range(8):
                j0 = pl.multiple_of(b * 128 + zz * (NY * NC * 2) + g * 8, 8)
                bias_f[pl.ds(j0, 8), t * 128 : (t + 1) * 128] = stage[
                    pl.ds(g * 64 + t, 8, stride=8), :
                ]
        return carry

    lax.fori_loop(0, 4 * nz, lay, 0)
    lane = lax.broadcasted_iota(jnp.int32, (16, length), 1)
    line = lax.broadcasted_iota(jnp.int32, (16, length), 0)
    for i in range(rows_dev):
        scaled = qc[0, i].astype(F32) * (factor * LOG2E)
        hi = scaled.astype(BF)
        rest = scaled - hi.astype(F32)
        mid = rest.astype(BF)
        low = (rest - mid.astype(F32)).astype(BF)
        ones = jnp.where(lax.broadcasted_iota(jnp.int32, (32, mine), 0) == 0, 1.0, 0.0).astype(BF)
        q3[i] = jnp.concatenate([hi, mid, low, ones], axis=0).T
        cs[i] = qc[1, i].T
        keys = kv[0, i]
        for n in range(3):
            k3[i, n * dim : (n + 1) * dim] = keys
        hidden = jnp.where((line == 0) & (lane >= lengths[i]), -1e30, 0.0).astype(BF)
        k3[i, 3 * dim : 3 * dim + 16] = hidden
        k3[i, 3 * dim + 16 :] = jnp.zeros((dim - 16, length), BF)
    acc[...] = jnp.zeros_like(acc)
    total[...] = jnp.zeros_like(total)

    def step(n, carry):
        jt, i = n // rows_dev, n % rows_dev
        rows = pl.ds(pl.multiple_of(jt * tile, tile), tile)
        s = jnp.dot(q3[i, rows], k3[i], preferred_element_type=F32) + bias_f[rows]
        p = jnp.exp2(s - jnp.max(s, axis=1, keepdims=True))
        w = p * (1.0 / jnp.sum(p, axis=1, keepdims=True))
        gw = jnp.dot(cs[i, rows], kv[1, i], preferred_element_type=F32)
        g = w * (gw - jnp.sum(w * gw, axis=1, keepdims=True))
        total[rows] += g
        gl = g.astype(BF)
        gq[i, :, rows] = (
            lax.dot_general(
                kv[0, i], gl, (((1,), (1,)), ((), ())), preferred_element_type=F32
            )
            * factor
        ).astype(BF)
        acc[0, i] += jnp.dot(qc[0, i, :, rows], gl, preferred_element_type=F32)
        acc[1, i] += jnp.dot(qc[1, i, :, rows], w.astype(BF), preferred_element_type=F32)
        return carry

    lax.fori_loop(0, rows_dev * (mine // tile), step, 0)
    for i in range(rows_dev):
        dkv[0, i] = (acc[0, i] * factor).astype(BF)
        dkv[1, i] = acc[1, i].astype(BF)

    def unlay(n, carry):
        b, zz = n // nz, n % nz
        for g in range(groups):
            for t in range(8):
                j0 = pl.multiple_of(b * 128 + zz * (NY * NC * 2) + g * 8, 8)
                stage[pl.ds(g * 64 + t, 8, stride=8), :] = total[
                    pl.ds(j0, 8), t * 128 : (t + 1) * 128
                ]
        gb[zz, :, :, b] = stage[...].reshape(NY, NC, 16, 128).astype(BF)
        return carry

    lax.fori_loop(0, 4 * nz, unlay, 0)


def scatter_kernel(
    nz, dkv, gq, gb, oq, ok, ov, ob, sum1, sum2a, sum2b, sum3, rk, rq, r1, r2a, r2b, r3a, r3b,
    s1, q1, s2a, q2a, s2b, q2b, s3a, q3a, s3b, q3b, s4, q4, skv, qkv, sq, qq, loc,
):
    row, key, a, x, z, y, core = place()
    rows_dev = dkv.shape[1]
    greet(nz)
    swap = remote(gb.at[:, :, 1 - core], r1, s1, q1, 0, (row_of(z, y, 1 - core), key))
    swap.start()
    others = []
    for s in range(1, NA * NX):
        to = lax.rem(key + s, NA * NX)
        cp = remote(
            dkv.at[:, :, :, pl.ds(to * 128, 128)], rk.at[key], skv, qkv, s - 1, (row, to)
        )
        cp.start()
        others.append(cp)
    for s in range(1, NX):
        to = lax.rem(x + s, NX)
        cp = remote(
            gq.at[:, :, pl.ds(to * 128, 128)], rq.at[x], sq, qq, s - 1, (row, a * NX + to)
        )
        cp.start()
        others.append(cp)
    mine = [
        pltpu.make_async_copy(dkv.at[:, :, :, pl.ds(key * 128, 128)], rk.at[key], loc.at[0]),
        pltpu.make_async_copy(gq.at[:, :, pl.ds(x * 128, 128)], rq.at[x], loc.at[1]),
    ]
    for cp in mine:
        cp.start()
    swap.wait()

    def join(n, carry):
        sum1[n] = (gb[n, :, core].astype(F32) + r1[n].astype(F32)).astype(BF)
        return carry

    lax.fori_loop(0, nz, join, 0)
    phase2a, phase2b = [], []
    for s in range(1, NY):
        to = lax.rem(y + s, NY)
        cp = remote(sum1.at[:, to, 0:2], r2a.at[s - 1], s2a, q2a, s - 1, (row_of(z, to, core), key))
        cp.start()
        phase2a.append(cp)
    for s in range(1, nz):
        to = lax.rem(z + s, nz)
        cp = remote(sum1.at[to, :, 2:4], r2b.at[s - 1], s2b, q2b, s - 1, (row_of(to, y, core), key))
        cp.start()
        phase2b.append(cp)
    phase3 = []
    for cp in phase2a:
        cp.wait()
    part = sum1[:, y, 0:2].astype(F32)
    for s in range(NY - 1):
        part += r2a[s].astype(F32)
    sum2a[...] = part.astype(BF)
    for s in range(1, nz):
        to = lax.rem(z + s, nz)
        cp = remote(sum2a.at[to], r3a.at[s - 1], s3a, q3a, s - 1, (row_of(to, y, core), key))
        cp.start()
        phase3.append(cp)
    for cp in phase2b:
        cp.wait()
    part = sum1[z, :, 2:4].astype(F32)
    for s in range(nz - 1):
        part += r2b[s].astype(F32)
    sum2b[...] = part.astype(BF)
    for s in range(1, NY):
        to = lax.rem(y + s, NY)
        cp = remote(sum2b.at[to], r3b.at[s - 1], s3b, q3b, s - 1, (row_of(z, to, core), key))
        cp.start()
        phase3.append(cp)
    for cp in phase3:
        cp.wait()
    part = sum2a[z].astype(F32)
    for s in range(nz - 1):
        part += r3a[s].astype(F32)
    sum3[0:2] = part
    part = sum2b[y].astype(F32)
    for s in range(NY - 1):
        part += r3b[s].astype(F32)
    sum3[2:4] = part
    last = []
    for s in range(1, NX):
        to = lax.rem(x + s, NX)
        cp = remote(sum3.at[to], ob.at[x], s4, q4, s - 1, (row, a * NX + to))
        cp.start()
        last.append(cp)
    ob[x] = sum3[x]
    for cp in mine + others:
        cp.wait()
    for i in range(rows_dev):
        oq[i] = jnp.concatenate([rq[h, i] for h in range(NX)], axis=0).T
        for part, out in enumerate((ok, ov)):
            both = [
                rk[h, part, i].astype(F32) + rk[NX + h, part, i].astype(F32) for h in range(NX)
            ]
            out[i] = jnp.concatenate(both, axis=0).astype(BF).T
    for cp in last:
        cp.wait()


def dma(*shape):
    return pltpu.SemaphoreType.DMA(shape)


def per_device(queries, keys_in, values, cotangent, pair_bias, key_lengths):
    rows_dev, block, feature = queries.shape
    heads, owned, length = pair_bias.shape
    dim = feature // heads
    nz = lax.axis_size("row") // (NY * NC)
    piece = (owned * length // 128, 128)
    mine = NX * block
    vmem = pl.BlockSpec(memory_space=VM)
    limit = 56 * 1024 * 1024
    kv_type = jax.ShapeDtypeStruct((2, rows_dev, dim, length), BF)
    qc_type = jax.ShapeDtypeStruct((2, rows_dev, dim, mine), BF)
    bg_type = jax.ShapeDtypeStruct((nz, NY, NC, NX) + piece, BF)

    def pairs(*counts):
        return [dma(n) for n in counts for _ in range(2)]

    kv, qc, bg = pl.pallas_call(
        lambda *refs: gather_kernel(nz, *refs),
        out_shape=(kv_type, qc_type, bg_type),
        in_specs=[vmem] * 5,
        out_specs=(vmem,) * 3,
        scratch_shapes=[
            VM((NX,) + piece, BF),
            VM((NX, 2, rows_dev, dim, block), BF),
            VM((NX, 2, rows_dev, dim, block), BF),
        ]
        + pairs(NX - 1, nz - 1, NY - 1, NY - 1, nz - 1, NY + nz, NA * NX - 1, NX - 1)
        + [dma(2)],
        compiler_params=pltpu.CompilerParams(
            collective_id=0, has_side_effects=True, vmem_limit_bytes=limit
        ),
        name="gather",
    )(queries, keys_in, values, cotangent, pair_bias.reshape((heads,) + piece))

    dkv, gq, gb = pl.pallas_call(
        lambda *refs: tile_kernel(nz, *refs),
        out_shape=(kv_type, jax.ShapeDtypeStruct((rows_dev, dim, mine), BF), bg_type),
        in_specs=[pl.BlockSpec(memory_space=pltpu.SMEM)] + [vmem] * 3,
        out_specs=(vmem,) * 3,
        scratch_shapes=[
            VM((rows_dev, mine, 4 * dim), BF),
            VM((rows_dev, 4 * dim, length), BF),
            VM((rows_dev, mine, dim), BF),
            VM((mine, length), F32),
            VM((mine, length), F32),
            VM((NY * NC * piece[0], 128), F32),
            VM((2, rows_dev, dim, length), F32),
        ],
        compiler_params=pltpu.CompilerParams(vmem_limit_bytes=limit),
        name="tiles",
    )(key_lengths, kv, qc, bg)

    kind = jax.ShapeDtypeStruct(queries.shape, BF)
    gq, gk, gv, gbias = pl.pallas_call(
        lambda *refs: scatter_kernel(nz, *refs),
        out_shape=(kind, kind, kind, jax.ShapeDtypeStruct((heads,) + piece, F32)),
        in_specs=[vmem] * 3,
        out_specs=(vmem,) * 4,
        scratch_shapes=[
            VM((nz, NY, NX) + piece, BF),
            VM((nz, 2) + piece, BF),
            VM((NY, 2) + piece, BF),
            VM((NX,) + piece, F32),
            VM((NA * NX, 2, rows_dev, dim, block), BF),
            VM((NX, rows_dev, dim, block), BF),
            VM((nz, NY, NX) + piece, BF),
            VM((NY - 1, nz, 2) + piece, BF),
            VM((nz - 1, NY, 2) + piece, BF),
            VM((nz - 1, 2) + piece, BF),
            VM((NY - 1, 2) + piece, BF),
        ]
        + pairs(1, NY - 1, nz - 1, nz - 1, NY - 1, NX - 1, NA * NX - 1, NX - 1)
        + [dma(2)],
        compiler_params=pltpu.CompilerParams(
            collective_id=1, has_side_effects=True, vmem_limit_bytes=limit
        ),
        name="scatter",
    )(dkv, gq, gb)
    return gq, gk, gv, gbias.reshape(pair_bias.shape)


def solution(mesh):
    wide = P("row", "key", None)
    bias = P(None, ("key", "row"), None)
    return jax.shard_map(
        per_device,
        mesh=mesh,
        in_specs=(wide, wide, wide, wide, bias, P("row")),
        out_specs=(wide, wide, wide, bias),
        check_vma=False,
    )
```

```python
import math

import jax
import jax.numpy as jnp
from jax import lax
from jax.experimental import pallas as pl
from jax.experimental.pallas import tpu as pltpu
from jax.sharding import PartitionSpec as P

MESH = pl.DeviceIdType.MESH
VM = pltpu.VMEM
BF = jnp.bfloat16
F32 = jnp.float32
NX, NA = 4, 2
NY, NC = 8, 2
LOG2E = 1.4426950408889634


def place():
    row, key = lax.axis_index("row"), lax.axis_index("key")
    return (
        row,
        key,
        lax.div(key, NX),
        lax.rem(key, NX),
        lax.div(row, NY * NC),
        lax.rem(lax.div(row, NC), NY),
        lax.rem(row, NC),
    )


def row_of(z, y, core):
    return (z * NY + y) * NC + core


def peers_of(nz):
    row, key, a, x, z, y, core = place()
    peers = [(row, lax.rem(key + s, NA * NX)) for s in range(1, NA * NX)]
    peers += [(row_of(lax.rem(z + s, nz), y, core), key) for s in range(1, nz)]
    peers += [(row_of(z, lax.rem(y + s, NY), core), key) for s in range(1, NY)]
    peers += [(row_of(z, y, 1 - core), key)]
    return peers


def remote(src, dst, sems, index, peer):
    return pltpu.make_async_remote_copy(
        src_ref=src,
        dst_ref=dst,
        send_sem=sems[0].at[index],
        recv_sem=sems[1].at[index],
        device_id=peer,
        device_id_type=MESH,
    )


def start(copies):
    for cp in copies:
        cp.start()
    return copies


def wait(copies):
    for cp in copies:
        cp.wait()


def kernel(
    nz, lengths, q, k, v, c, bias, oq, ok, ov, ob,
    pieces, own, bg, kvs, qcs, kv, qc, q3, k3, cs, stage, eb, e, gws, total, acc, dkv, gq,
    gbs, r1, s1, r2a, r2b, s2a, s2b, r3a, r3b, s3, r4, rk, rq, loc, *pairs,
):
    row, key, a, x, z, y, core = place()
    rows_dev, block, feature = q.shape
    length = bias.shape[2]
    dim = feature // NX
    factor = 1.0 / math.sqrt(dim)
    sems = [(pairs[n], pairs[n + 1]) for n in range(0, len(pairs), 2)]
    m0, m1a, m1b, m2, m3, mkv, mqc, n1, n2, n3, n4, nkv, ngq = sems
    partner = (row_of(z, y, 1 - core), key)

    def y_peer(s):
        return (row_of(z, lax.rem(y + s, NY), core), key)

    def z_peer(s):
        return (row_of(lax.rem(z + s, nz), y, core), key)

    def x_peer(s):
        return (row, a * NX + lax.rem(x + s, NX))

    barrier = pltpu.get_barrier_semaphore()
    peers = peers_of(nz)
    for peer in peers:
        pl.semaphore_signal(barrier, inc=1, device_id=peer, device_id_type=MESH)

    for h in range(NX):
        lines = bias[h].astype(F32)
        for j in range(2):
            for t in range(8):
                n = h * 16 + j * 8 + t
                stage[n : n + 1, :] = lines[j : j + 1, t * 128 : (t + 1) * 128]
    for h in range(NX):
        pieces[h] = stage[h * 16 : (h + 1) * 16, :].astype(BF)
    for held, sources in ((kvs, (k, v)), (qcs, (q, c))):
        for part, source in enumerate(sources):
            for i in range(rows_dev):
                turned = source[i].T
                for h in range(NX):
                    held[h, part, i] = turned[h * dim : (h + 1) * dim]
    own[x] = pieces[x]
    pl.semaphore_wait(barrier, len(peers))

    first = start(
        [remote(pieces.at[lax.rem(x + s, NX)], own.at[x], m0, s - 1, x_peer(s)) for s in range(1, NX)]
    )
    others = []
    for s in range(1, NA * NX):
        to = lax.rem(key + s, NA * NX)
        others.append(
            remote(
                kvs.at[lax.rem(to, NX)], kv.at[:, :, :, pl.ds(key * 128, 128)], mkv, s - 1, (row, to)
            )
        )
    for s in range(1, NX):
        to = lax.rem(x + s, NX)
        others.append(
            remote(qcs.at[to], qc.at[:, :, :, pl.ds(x * 128, 128)], mqc, s - 1, x_peer(s))
        )
    start(others)
    mine = start(
        [
            pltpu.make_async_copy(kvs.at[x], kv.at[:, :, :, pl.ds(key * 128, 128)], loc.at[0]),
            pltpu.make_async_copy(qcs.at[x], qc.at[:, :, :, pl.ds(x * 128, 128)], loc.at[1]),
        ]
    )
    wait(first)
    phase1a = start(
        [
            remote(own.at[0:2], bg.at[0:2, core, z, y], m1a, s - 1, z_peer(s))
            for s in range(1, nz)
        ]
    )
    phase1b = start(
        [
            remote(own.at[2:4], bg.at[2:4, core, z, y], m1b, s - 1, y_peer(s))
            for s in range(1, NY)
        ]
    )
    for b in range(NX):
        bg[b, core, z, y] = own[b]
    phase2 = {}

    def spread(b):
        if b < 2:
            piece = bg.at[b, core, :, y]
            phase2[b] = [remote(piece, piece, m2, b * 7 + s - 1, y_peer(s)) for s in range(1, NY)]
        else:
            piece = bg.at[b, core, z]
            phase2[b] = [remote(piece, piece, m2, b * 7 + s - 1, z_peer(s)) for s in range(1, nz)]
        start(phase2[b])

    wait(phase1a)
    spread(0)
    wait(phase1b)
    spread(2)
    spread(3)
    spread(1)

    wait(mine + others)
    lane = lax.broadcasted_iota(jnp.int32, (16, length), 1)
    line = lax.broadcasted_iota(jnp.int32, (16, length), 0)
    span = NX * block
    for i in range(rows_dev):
        scaled = qc[0, i].astype(F32) * (factor * LOG2E)
        hi = scaled.astype(BF)
        rest = scaled - hi.astype(F32)
        mid = rest.astype(BF)
        low = (rest - mid.astype(F32)).astype(BF)
        ones = jnp.where(lax.broadcasted_iota(jnp.int32, (dim, span), 0) == 0, 1.0, 0.0).astype(BF)
        q3[i] = jnp.concatenate([hi, mid, low, ones], axis=0).T
        cs[i] = qc[1, i].T
        for n in range(3):
            k3[i, n * dim : (n + 1) * dim] = kv[0, i]
        hidden = jnp.where((line == 0) & (lane >= lengths[i]), -1e30, 0.0).astype(BF)
        k3[i, 3 * dim : 3 * dim + 16] = hidden
        k3[i, 3 * dim + 16 :] = jnp.zeros((dim - 16, length), BF)

    def early(n, carry):
        i, half = n // 2, n % 2
        rows = pl.ds(pl.multiple_of(half * 256, 256), 256)
        s = jnp.dot(q3[i, rows], k3[i], preferred_element_type=F32)
        e[i, rows] = jnp.exp2(s - jnp.max(s, axis=1, keepdims=True))
        gws[i, rows] = jnp.dot(cs[i, rows], kv[1, i], preferred_element_type=F32)
        return carry

    lax.fori_loop(0, 2 * rows_dev, early, 0)
    acc[...] = jnp.zeros_like(acc)
    total[...] = jnp.zeros_like(total)

    swaps = {}

    def hand(b):
        wait(phase2[b])
        swaps[b] = start([remote(bg.at[b, core], bg.at[b, core], m3, b, partner)])

    def lay(b):
        def part(zz, carry):
            for g in range(NY * NC):
                stage[g * 16 : (g + 1) * 16, :] = bg[b, g % NC, zz, g // NC].astype(F32) * LOG2E
            for g in range(NY * NC // 4):
                for t in range(8):
                    j0 = pl.multiple_of(b * block + zz * (NY * NC * 2) + g * 8, 8)
                    eb[pl.ds(j0, 8), t * 128 : (t + 1) * 128] = jnp.exp2(
                        stage[pl.ds(g * 64 + t, 8, stride=8), :]
                    )
            return carry

        lax.fori_loop(0, nz, part, 0)

    def late(b):
        rows = slice(b * block, (b + 1) * block)

        def one(i, carry):
            p = e[i, rows] * eb[rows]
            gw = gws[i, rows]
            inv = 1.0 / jnp.sum(p, axis=1, keepdims=True)
            w = p * inv
            g = w * (gw - jnp.sum(p * gw, axis=1, keepdims=True) * inv)
            total[rows] += g
            gl = g.astype(BF)
            gq[i, :, rows] = (
                lax.dot_general(
                    kv[0, i], gl, (((1,), (1,)), ((), ())), preferred_element_type=F32
                )
                * factor
            ).astype(BF)
            acc[0, i] += jnp.dot(qc[0, i, :, rows], gl, preferred_element_type=F32)
            acc[1, i] += jnp.dot(qc[1, i, :, rows], w.astype(BF), preferred_element_type=F32)
            return carry

        lax.fori_loop(0, rows_dev, one, 0, unroll=2)

    def unlay(b):
        def part(zz, carry):
            for g in range(NY * NC // 4):
                for t in range(8):
                    j0 = pl.multiple_of(b * block + zz * (NY * NC * 2) + g * 8, 8)
                    stage[pl.ds(g * 64 + t, 8, stride=8), :] = total[
                        pl.ds(j0, 8), t * 128 : (t + 1) * 128
                    ]
            for g in range(NY * NC):
                gbs[b, g % NC, zz, g // NC] = stage[g * 16 : (g + 1) * 16, :].astype(BF)
            return carry

        lax.fori_loop(0, nz, part, 0)

    flying = {}

    def swap(b):
        flying[1, b] = start([remote(gbs.at[b, 1 - core], r1.at[b], n1, b, partner)])

    def join(b):
        wait(flying[1, b])
        s1[b] = (gbs[b, core].astype(F32) + r1[b].astype(F32)).astype(BF)
        if b < 2:
            copies = [
                remote(s1.at[b, :, lax.rem(y + s, NY)], r2a.at[b, s - 1], n2, b * 7 + s - 1, y_peer(s))
                for s in range(1, NY)
            ]
        else:
            copies = [
                remote(s1.at[b, lax.rem(z + s, nz)], r2b.at[b - 2, s - 1], n2, b * 7 + s - 1, z_peer(s))
                for s in range(1, nz)
            ]
        flying[2, b] = start(copies)

    def second(b):
        wait(flying[2, b])
        if b < 2:
            part = s1[b, :, y].astype(F32)
            for s in range(NY - 1):
                part += r2a[b, s].astype(F32)
            s2a[b] = part.astype(BF)
            copies = [
                remote(s2a.at[b, lax.rem(z + s, nz)], r3a.at[b, s - 1], n3, b * 7 + s - 1, z_peer(s))
                for s in range(1, nz)
            ]
        else:
            part = s1[b, z].astype(F32)
            for s in range(nz - 1):
                part += r2b[b - 2, s].astype(F32)
            s2b[b - 2] = part.astype(BF)
            copies = [
                remote(s2b.at[b - 2, lax.rem(y + s, NY)], r3b.at[b - 2, s - 1], n3, b * 7 + s - 1, y_peer(s))
                for s in range(1, NY)
            ]
        flying[3, b] = start(copies)

    def third(b):
        wait(flying[3, b])
        if b < 2:
            part = s2a[b, z].astype(F32)
            for s in range(nz - 1):
                part += r3a[b, s].astype(F32)
        else:
            part = s2b[b - 2, y].astype(F32)
            for s in range(NY - 1):
                part += r3b[b - 2, s].astype(F32)
        s3[b] = part

    order = (0, 2, 3, 1)
    hand(0)
    hand(2)
    for n, b in enumerate(order):
        if n == 1:
            hand(3)
        if n == 2:
            hand(1)
        wait(swaps[b])
        lay(b)
        late(b)
        unlay(b)
        swap(b)
        if n >= 1:
            join(order[n - 1])
        if n >= 2:
            second(order[n - 2])

    for i in range(rows_dev):
        dkv[0, i] = (acc[0, i] * factor).astype(BF)
        dkv[1, i] = acc[1, i].astype(BF)
    outs = []
    for s in range(1, NA * NX):
        to = lax.rem(key + s, NA * NX)
        outs.append(
            remote(dkv.at[:, :, :, pl.ds(to * 128, 128)], rk.at[key], nkv, s - 1, (row, to))
        )
    for s in range(1, NX):
        to = lax.rem(x + s, NX)
        outs.append(remote(gq.at[:, :, pl.ds(to * 128, 128)], rq.at[x], ngq, s - 1, x_peer(s)))
    start(outs)
    held = start(
        [
            pltpu.make_async_copy(dkv.at[:, :, :, pl.ds(key * 128, 128)], rk.at[key], loc.at[2]),
            pltpu.make_async_copy(gq.at[:, :, pl.ds(x * 128, 128)], rq.at[x], loc.at[3]),
        ]
    )
    join(order[3])
    second(order[2])
    third(order[0])
    second(order[3])
    third(order[1])
    third(order[2])
    third(order[3])
    last = start(
        [
            remote(s3.at[lax.rem(x + s, NX)], r4.at[x], n4, s - 1, x_peer(s))
            for s in range(1, NX)
        ]
    )
    r4[x] = s3[x]
    wait(held + outs)
    for i in range(rows_dev):
        oq[i] = jnp.concatenate([rq[h, i] for h in range(NX)], axis=0).T
        for part, out in enumerate((ok, ov)):
            both = [
                rk[h, part, i].astype(F32) + rk[NX + h, part, i].astype(F32) for h in range(NX)
            ]
            out[i] = jnp.concatenate(both, axis=0).astype(BF).T
    wait(last)
    for h in range(NX):
        for j in range(2):
            for t in range(8):
                n = j * 8 + t
                ob[h, j : j + 1, t * 128 : (t + 1) * 128] = r4[h, n : n + 1, :]


def dma(*shape):
    return pltpu.SemaphoreType.DMA(shape)


def per_device(queries, keys_in, values, cotangent, pair_bias, key_lengths):
    rows_dev, block, feature = queries.shape
    heads, owned, length = pair_bias.shape
    dim = feature // heads
    nz = lax.axis_size("row") // (NY * NC)
    tile = (owned * length // 128, 128)
    span = NX * block
    vmem = pl.BlockSpec(memory_space=VM)
    kind = jax.ShapeDtypeStruct(queries.shape, BF)
    scratch = [
        VM((NX,) + tile, BF),
        VM((NX,) + tile, BF),
        VM((NX, NC, nz, NY) + tile, BF),
        VM((NX, 2, rows_dev, dim, block), BF),
        VM((NX, 2, rows_dev, dim, block), BF),
        VM((2, rows_dev, dim, length), BF),
        VM((2, rows_dev, dim, span), BF),
        VM((rows_dev, span, 4 * dim), BF),
        VM((rows_dev, 4 * dim, length), BF),
        VM((rows_dev, span, dim), BF),
        VM((NY * NC * tile[0], 128), F32),
        VM((span, length), F32),
        VM((rows_dev, span, length), F32),
        VM((rows_dev, span, length), F32),
        VM((span, length), F32),
        VM((2, rows_dev, dim, length), F32),
        VM((2, rows_dev, dim, length), BF),
        VM((rows_dev, dim, span), BF),
        VM((NX, NC, nz, NY) + tile, BF),
        VM((NX, nz, NY) + tile, BF),
        VM((NX, nz, NY) + tile, BF),
        VM((2, NY - 1, nz) + tile, BF),
        VM((2, nz - 1, NY) + tile, BF),
        VM((2, nz) + tile, BF),
        VM((2, NY) + tile, BF),
        VM((2, nz - 1) + tile, BF),
        VM((2, NY - 1) + tile, BF),
        VM((NX,) + tile, F32),
        VM((NX,) + tile, F32),
        VM((NA * NX, 2, rows_dev, dim, block), BF),
        VM((NX, rows_dev, dim, block), BF),
        dma(4),
    ]
    counts = (NX - 1, nz - 1, NY - 1, 28, NX, NA * NX - 1, NX - 1)
    counts += (NX, 28, 28, NX - 1, NA * NX - 1, NX - 1)
    scratch += [dma(n) for n in counts for _ in range(2)]
    return pl.pallas_call(
        lambda *refs: kernel(nz, *refs),
        out_shape=(kind, kind, kind, jax.ShapeDtypeStruct(pair_bias.shape, F32)),
        in_specs=[pl.BlockSpec(memory_space=pltpu.SMEM)] + [vmem] * 5,
        out_specs=(vmem,) * 4,
        scratch_shapes=scratch,
        compiler_params=pltpu.CompilerParams(
            collective_id=0, has_side_effects=True, vmem_limit_bytes=60 * 1024 * 1024
        ),
        name="attention_grad",
    )(key_lengths, queries, keys_in, values, cotangent, pair_bias)


def solution(mesh):
    wide = P("row", "key", None)
    bias = P(None, ("key", "row"), None)
    return jax.shard_map(
        per_device,
        mesh=mesh,
        in_specs=(wide, wide, wide, wide, bias, P("row")),
        out_specs=(wide, wide, wide, bias),
        check_vma=False,
    )
```

```python
import math

import jax
import jax.numpy as jnp
from jax import lax
from jax.experimental import pallas as pl
from jax.experimental.pallas import tpu as pltpu
from jax.sharding import PartitionSpec as P

MESH = pl.DeviceIdType.MESH
VM = pltpu.VMEM
BF = jnp.bfloat16
F32 = jnp.float32
NX, NA = 4, 2
NY, NC = 8, 2
LOG2E = 1.4426950408889634


def place():
    row, key = lax.axis_index("row"), lax.axis_index("key")
    return (
        row,
        key,
        lax.div(key, NX),
        lax.rem(key, NX),
        lax.div(row, NY * NC),
        lax.rem(lax.div(row, NC), NY),
        lax.rem(row, NC),
    )


def row_of(z, y, core):
    return (z * NY + y) * NC + core


def remote(src, dst, sems, out, back, peer):
    return pltpu.make_async_remote_copy(
        src_ref=src,
        dst_ref=dst,
        send_sem=sems[0].at[out],
        recv_sem=sems[1].at[back],
        device_id=peer,
        device_id_type=MESH,
    )


def start(copies):
    for cp in copies:
        cp.start()
    return copies


def wait(copies):
    for cp in copies:
        cp.wait()


def far_first(n):
    return sorted(range(1, n), key=lambda s: -min(s, n - s))


def kernel(
    nz, lengths, q, k, v, c, bias, rq, ks, r4,
    pieces, own, bg, kvs, qcs, kv, qc, lens, stage, eb, e, gws, total, acc, dkv, gq, rd,
    sd, gbs, r2a, r2b, s2a, s2b, r3a, r3b, s3, rk, loc, *pairs,
):
    row, key, a, x, z, y, core = place()
    rows_dev, block, feature = q.shape
    length = bias.shape[2]
    dim = feature // NX
    factor = 1.0 / math.sqrt(dim)
    sems = [(pairs[n], pairs[n + 1]) for n in range(0, len(pairs), 2)]
    m0, m1a, m1b, m2a, m2b, mkv, mqc, mswap, n2a, n2b, n3a, n3b, n4, nkv, ngq, nswap, mlen = sems
    other = row_of(z, y, 1 - core)
    half = lax.div(x, 2)
    side = lax.rem(x, 2)
    here = half == core

    def y_peer(s):
        return (row_of(z, lax.rem(y + s, NY), core), key)

    def z_peer(s):
        return (row_of(lax.rem(z + s, nz), y, core), key)

    ys, zs, xs = far_first(NY), far_first(nz), far_first(NX)
    barrier = pltpu.get_barrier_semaphore()
    peers = [(row, lax.rem(key + s, NA * NX)) for s in range(1, NA * NX)]
    peers += [(other, a * NX + lax.rem(x + s, NX)) for s in range(NX)]
    peers += [z_peer(s) for s in zs] + [y_peer(s) for s in ys]
    for peer in peers:
        pl.semaphore_signal(barrier, inc=1, device_id=peer, device_id_type=MESH)

    for h in range(NX):
        lines = bias[h].astype(F32)
        for j in range(2):
            for t in range(8):
                n = h * 16 + j * 8 + t
                stage[n : n + 1, :] = lines[j : j + 1, t * 128 : (t + 1) * 128]
    for h in range(NX):
        pieces[h] = stage[h * 16 : (h + 1) * 16, :].astype(BF)
    for held, sources in ((kvs, (k, v)), (qcs, (q, c))):
        for part, source in enumerate(sources):
            for i in range(rows_dev):
                turned = source[i].T
                for h in range(NX):
                    held[h, part, i] = turned[h * dim : (h + 1) * dim]
    spots = lax.broadcasted_iota(jnp.int32, (8, 128), 0)
    known = jnp.zeros((8, 128), F32)
    for i in range(rows_dev):
        known = jnp.where(spots == i, lengths[i].astype(F32), known)
    lens[core] = known
    pl.semaphore_wait(barrier, len(peers))

    target = row_of(z, y, half)

    def heads(source, dest, sems):
        return [
            remote(
                source.at[lax.rem(x + s, NX)], dest, sems, s, side * NC + core,
                (target, a * NX + lax.rem(x + s, NX)),
            )
            for s in [2, 1, 3, 0]
        ]

    def arrivals(source, dest, sems):
        for b in range(2):
            for g in range(NC):
                mine = (x == core * 2 + b) & (core == g)

                @pl.when(jnp.logical_not(mine))
                def _():
                    remote(
                        source.at[0], dest(b, g), sems, 0, b * NC + g, (other, key)
                    ).wait_recv()

    def launch(copies):
        start(copies[:-1])
        pl.when(jnp.logical_not(here))(copies[-1].start)

    def sent(copies):
        for cp in copies[:-1]:
            cp.wait_send()
        pl.when(jnp.logical_not(here))(copies[-1].wait_send)

    first = heads(pieces, own.at[side, core], m0)
    launch(first)

    @pl.when(here)
    def _():
        own[side, core] = pieces[x]

    tell = start([remote(lens.at[core], lens.at[core], mlen, 0, 0, (other, key))])
    others = []
    for s in (6, 2, 5, 7, 1, 3, 4):
        to = lax.rem(key + s, NA * NX)
        others.append(
            remote(
                kvs.at[lax.rem(to, NX)], kv.at[core, :, :, :, pl.ds(key * 128, 128)],
                mkv, s - 1, s - 1, (row, to),
            )
        )
    start(others)
    mine = start(
        [pltpu.make_async_copy(kvs.at[x], kv.at[core, :, :, :, pl.ds(key * 128, 128)], loc.at[0])]
    )

    def qc_place(b, g):
        return qc.at[g, :, :, :, b * 128 : (b + 1) * 128]

    asks = heads(qcs, qc.at[core, :, :, :, pl.ds(side * 128, 128)], mqc)
    launch(asks)
    keep = pltpu.make_async_copy(
        qcs.at[x], qc.at[core, :, :, :, pl.ds(side * 128, 128)], loc.at[1]
    )
    pl.when(here)(keep.start)

    arrivals(pieces, lambda b, g: own.at[b, g], m0)
    phase1a = start([remote(own.at[0], bg.at[0, z, y], m1a, s - 1, s - 1, z_peer(s)) for s in zs])
    phase1b = start([remote(own.at[1], bg.at[1, z, y], m1b, s - 1, s - 1, y_peer(s)) for s in ys])
    for b in range(2):
        bg[b, z, y] = own[b]
    wait(phase1a)
    piece = bg.at[0, :, y]
    phase2a = start([remote(piece, piece, m2a, s - 1, s - 1, y_peer(s)) for s in ys])
    wait(phase1b)
    piece = bg.at[1, z]
    phase2b = start([remote(piece, piece, m2b, s - 1, s - 1, z_peer(s)) for s in zs])

    wait(mine + others)
    swap = start([remote(kv.at[core], kv.at[core], mswap, 0, 0, (other, key))])
    arrivals(qcs, qc_place, mqc)
    pl.when(here)(keep.wait)
    lane = lax.broadcasted_iota(jnp.int32, (16, length), 1).astype(F32)
    line = lax.broadcasted_iota(jnp.int32, (16, length), 0)
    span = 2 * block

    def early(n, carry):
        g, i = n // rows_dev, n % rows_dev
        scaled = qc[g, 0, i].astype(F32) * (factor * LOG2E)
        hi = scaled.astype(BF)
        rest = scaled - hi.astype(F32)
        mid = rest.astype(BF)
        low = (rest - mid.astype(F32)).astype(BF)
        ones = jnp.where(lax.broadcasted_iota(jnp.int32, (dim, span), 0) == 0, 1.0, 0.0).astype(BF)
        q3 = jnp.concatenate([hi, mid, low, ones], axis=0).T
        keys = kv[g, 0, i]
        valid = jnp.concatenate([lens[g, pl.ds(i, 1), :]] * (length // 128), axis=1)
        hidden = jnp.where((line == 0) & (lane >= valid), -1e30, 0.0).astype(BF)
        k3 = jnp.concatenate([keys, keys, keys, hidden, jnp.zeros_like(hidden)], axis=0)
        s = jnp.dot(q3, k3, preferred_element_type=F32)
        e[g, i] = jnp.exp2(s - jnp.max(s, axis=1, keepdims=True))
        gws[g, i] = jnp.dot(qc[g, 1, i].T, kv[g, 1, i], preferred_element_type=F32)
        return carry

    def early_rows(g):
        lax.fori_loop(g * rows_dev, (g + 1) * rows_dev, early, 0)

    early_rows(core)
    wait(swap + tell)
    early_rows(1 - core)
    acc[...] = jnp.zeros_like(acc)
    total[...] = jnp.zeros_like(total)

    def lay(b):
        def part(zz, carry):
            stage[...] = bg[b, zz].astype(F32).reshape(NY * NC * 16, 128) * LOG2E
            for g in range(NY * NC // 4):
                for t in range(8):
                    j0 = pl.multiple_of(b * block + zz * (NY * NC * 2) + g * 8, 8)
                    eb[pl.ds(j0, 8), t * 128 : (t + 1) * 128] = jnp.exp2(
                        stage[pl.ds(g * 64 + t, 8, stride=8), :]
                    )
            return carry

        lax.fori_loop(0, nz, part, 0)

    def late(b, g):
        rows = slice(b * block, (b + 1) * block)

        def one(i, carry):
            p = e[g, i, rows] * eb[rows]
            gw = gws[g, i, rows]
            inv = 1.0 / jnp.sum(p, axis=1, keepdims=True)
            w = p * inv
            grad = w * (gw - jnp.sum(p * gw, axis=1, keepdims=True) * inv)
            total[rows] += grad
            low = grad.astype(BF)
            gq[g, i, :, rows] = (
                lax.dot_general(
                    kv[g, 0, i], low, (((1,), (1,)), ((), ())), preferred_element_type=F32
                )
                * factor
            ).astype(BF)
            acc[g, 0, i] += jnp.dot(qc[g, 0, i, :, rows], low, preferred_element_type=F32)
            acc[g, 1, i] += jnp.dot(
                qc[g, 1, i, :, rows], w.astype(BF), preferred_element_type=F32
            )
            return carry

        lax.fori_loop(0, rows_dev, one, 0, unroll=2)

    def unlay(b):
        def part(zz, carry):
            for g in range(NY * NC // 4):
                for t in range(8):
                    j0 = pl.multiple_of(b * block + zz * (NY * NC * 2) + g * 8, 8)
                    stage[pl.ds(g * 64 + t, 8, stride=8), :] = total[
                        pl.ds(j0, 8), t * 128 : (t + 1) * 128
                    ]
            gbs[b, zz] = stage[...].reshape(NY, NC, 16, 128).astype(BF)
            return carry

        lax.fori_loop(0, nz, part, 0)

    wait(phase2a)
    lay(0)
    late(0, 1 - core)
    late(0, core)
    unlay(0)
    sum2a = start(
        [
            remote(gbs.at[0, :, lax.rem(y + s, NY)], r2a.at[s - 1], n2a, s - 1, s - 1, y_peer(s))
            for s in ys
        ]
    )
    wait(phase2b)
    lay(1)
    late(1, 1 - core)
    for i in range(rows_dev):
        dkv[1 - core, 0, i] = (acc[1 - core, 0, i] * factor).astype(BF)
        dkv[1 - core, 1, i] = acc[1 - core, 1, i].astype(BF)
    give = start([remote(dkv.at[1 - core], rd, nswap, 0, 0, (other, key))])
    late(1, core)
    unlay(1)
    sum2b = start(
        [
            remote(gbs.at[1, lax.rem(z + s, nz)], r2b.at[s - 1], n2b, s - 1, s - 1, z_peer(s))
            for s in zs
        ]
    )

    backs = []
    for b in range(2):
        for g in range(NC):
            away = jnp.logical_not((x == core * 2 + b) & (core == g))
            piece = gq.at[g, :, :, b * 128 : (b + 1) * 128]
            owner = (row_of(z, y, g), a * NX + core * 2 + b)
            cp = remote(piece, rq.at[x], ngq, b * NC + g, x, owner)
            pl.when(away)(cp.start)
            keep = pltpu.make_async_copy(piece, rq.at[x], loc.at[2])
            pl.when(jnp.logical_not(away))(keep.start)
            backs.append((away, cp, keep))
    wait(give)
    for i in range(rows_dev):
        sd[0, i] = (acc[core, 0, i] * factor + rd[0, i].astype(F32)).astype(BF)
        sd[1, i] = (acc[core, 1, i] + rd[1, i].astype(F32)).astype(BF)
    outs = []
    for s in (6, 2, 5, 7, 1, 3, 4):
        to = lax.rem(key + s, NA * NX)
        outs.append(
            remote(
                sd.at[:, :, :, pl.ds(to * 128, 128)], rk.at[key], nkv, s - 1, s - 1, (row, to)
            )
        )
    start(outs)
    held = start(
        [pltpu.make_async_copy(sd.at[:, :, :, pl.ds(key * 128, 128)], rk.at[key], loc.at[3])]
    )

    wait(sum2a)
    part = gbs[0, :, y].astype(F32)
    for s in range(NY - 1):
        part += r2a[s].astype(F32)
    s2a[...] = part.astype(BF)
    sum3a = start(
        [
            remote(s2a.at[lax.rem(z + s, nz)], r3a.at[s - 1], n3a, s - 1, s - 1, z_peer(s))
            for s in zs
        ]
    )
    wait(sum2b)
    part = gbs[1, z].astype(F32)
    for s in range(nz - 1):
        part += r2b[s].astype(F32)
    s2b[...] = part.astype(BF)
    sum3b = start(
        [
            remote(s2b.at[lax.rem(y + s, NY)], r3b.at[s - 1], n3b, s - 1, s - 1, y_peer(s))
            for s in ys
        ]
    )
    wait(sum3a)
    part = s2a[z].astype(F32)
    for s in range(nz - 1):
        part += r3a[s].astype(F32)
    s3[0] = part
    wait(sum3b)
    part = s2b[y].astype(F32)
    for s in range(NY - 1):
        part += r3b[s].astype(F32)
    s3[1] = part
    ends = []
    for b in range(2):
        for g in range(NC):
            away = jnp.logical_not((x == core * 2 + b) & (core == g))
            owner = (row_of(z, y, g), a * NX + core * 2 + b)
            cp = remote(s3.at[b, g], r4.at[x], n4, b * NC + g, x, owner)
            pl.when(away)(cp.start)
            ends.append((away, cp))

    @pl.when(here)
    def _():
        r4[x] = s3[side, core]

    wait(held + outs)
    for i in range(rows_dev):
        for part in range(2):
            for h in range(NX):
                ks[part, i, h * dim : (h + 1) * dim] = (
                    rk[h, part, i].astype(F32) + rk[NX + h, part, i].astype(F32)
                ).astype(BF)
    for away, cp, keep in backs:
        pl.when(away)(cp.wait_send)
        pl.when(jnp.logical_not(away))(keep.wait)
    for away, cp in ends:
        pl.when(away)(cp.wait_send)
    sent(first)
    sent(asks)
    for h in range(NX):

        @pl.when(jnp.logical_not((x == h) & here))
        def _():
            remote(gq.at[0, :, :, 0:128], rq.at[h], ngq, 0, h, (other, key)).wait_recv()
            remote(s3.at[0, 0], r4.at[h], n4, 0, h, (other, key)).wait_recv()


def finish(rq, ks, r4, oq, ok, ov, ob):
    for i in range(oq.shape[0]):
        oq[i] = jnp.concatenate([rq[h, i] for h in range(NX)], axis=0).T
        ok[i] = ks[0, i].T
        ov[i] = ks[1, i].T
    for h in range(NX):
        for j in range(2):
            for t in range(8):
                n = j * 8 + t
                ob[h, j : j + 1, t * 128 : (t + 1) * 128] = r4[h, n : n + 1, :]


def dma(*shape):
    return pltpu.SemaphoreType.DMA(shape)


def per_device(queries, keys_in, values, cotangent, pair_bias, key_lengths):
    rows_dev, block, feature = queries.shape
    heads, owned, length = pair_bias.shape
    dim = feature // heads
    nz = lax.axis_size("row") // (NY * NC)
    tile = (owned * length // 128, 128)
    span = 2 * block
    vmem = pl.BlockSpec(memory_space=VM)
    kind = jax.ShapeDtypeStruct(queries.shape, BF)
    scratch = [
        VM((NX,) + tile, BF),
        VM((2, NC) + tile, BF),
        VM((2, nz, NY, NC) + tile, BF),
        VM((NX, 2, rows_dev, dim, block), BF),
        VM((NX, 2, rows_dev, dim, block), BF),
        VM((NC, 2, rows_dev, dim, length), BF),
        VM((NC, 2, rows_dev, dim, span), BF),
        VM((NC, 8, 128), F32),
        VM((NY * NC * tile[0], 128), F32),
        VM((span, length), F32),
        VM((NC, rows_dev, span, length), F32),
        VM((NC, rows_dev, span, length), F32),
        VM((span, length), F32),
        VM((NC, 2, rows_dev, dim, length), F32),
        VM((NC, 2, rows_dev, dim, length), BF),
        VM((NC, rows_dev, dim, span), BF),
        VM((2, rows_dev, dim, length), BF),
        VM((2, rows_dev, dim, length), BF),
        VM((2, nz, NY, NC) + tile, BF),
        VM((NY - 1, nz, NC) + tile, BF),
        VM((nz - 1, NY, NC) + tile, BF),
        VM((nz, NC) + tile, BF),
        VM((NY, NC) + tile, BF),
        VM((nz - 1, NC) + tile, BF),
        VM((NY - 1, NC) + tile, BF),
        VM((2, NC) + tile, F32),
        VM((NA * NX, 2, rows_dev, dim, block), BF),
        dma(4),
    ]
    counts = (4, nz - 1, NY - 1, NY - 1, nz - 1, NA * NX - 1, 4, 1)
    counts += (NY - 1, nz - 1, nz - 1, NY - 1, 4, NA * NX - 1, 4, 1, 1)
    scratch += [dma(n) for n in counts for _ in range(2)]
    passed = (
        jax.ShapeDtypeStruct((NX, rows_dev, dim, block), BF),
        jax.ShapeDtypeStruct((2, rows_dev, feature, block), BF),
        jax.ShapeDtypeStruct((heads,) + tile, F32),
    )
    parts = pl.pallas_call(
        lambda *refs: kernel(nz, *refs),
        out_shape=passed,
        in_specs=[pl.BlockSpec(memory_space=pltpu.SMEM)] + [vmem] * 5,
        out_specs=(vmem,) * 3,
        scratch_shapes=scratch,
        compiler_params=pltpu.CompilerParams(
            collective_id=0, has_side_effects=True, vmem_limit_bytes=60 * 1024 * 1024
        ),
        name="attention_grad",
    )(key_lengths, queries, keys_in, values, cotangent, pair_bias)
    return pl.pallas_call(
        finish,
        out_shape=(kind, kind, kind, jax.ShapeDtypeStruct(pair_bias.shape, F32)),
        in_specs=[vmem] * 3,
        out_specs=(vmem,) * 4,
        compiler_params=pltpu.CompilerParams(vmem_limit_bytes=60 * 1024 * 1024),
        name="finish",
    )(*parts)


def solution(mesh):
    wide = P("row", "key", None)
    bias = P(None, ("key", "row"), None)
    return jax.shard_map(
        per_device,
        mesh=mesh,
        in_specs=(wide, wide, wide, wide, bias, P("row")),
        out_specs=(wide, wide, wide, bias),
        check_vma=False,
    )
```

```python
import math

import jax
import jax.numpy as jnp
from jax import lax
from jax.experimental import pallas as pl
from jax.experimental.pallas import tpu as pltpu
from jax.sharding import PartitionSpec as P

MESH = pl.DeviceIdType.MESH
VM = pltpu.VMEM
BF = jnp.bfloat16
F32 = jnp.float32
NX, NA = 4, 2
NY, NC = 8, 2
LOG2E = 1.4426950408889634
EXCHANGES = 21


def place():
    row, key = lax.axis_index("row"), lax.axis_index("key")
    return (
        row,
        key,
        lax.div(key, NX),
        lax.rem(key, NX),
        lax.div(row, NY * NC),
        lax.rem(lax.div(row, NC), NY),
        lax.rem(row, NC),
    )


def row_of(z, y, core):
    return (z * NY + y) * NC + core


def remote(src, dst, sems, peer):
    return pltpu.make_async_remote_copy(
        src_ref=src,
        dst_ref=dst,
        send_sem=sems[0],
        recv_sem=sems[1],
        device_id=peer,
        device_id_type=MESH,
    )


def take(sem, like):
    pltpu.make_async_copy(like, like, sem).wait()


def start(copies):
    for cp in copies:
        cp.start()
    return copies


def far_first(n):
    return sorted(range(1, n), key=lambda s: -min(s, n - s))


def kernel(
    nz, lengths, q, k, v, c, bias, rq, ks, r4,
    pieces, own, bg, kvs, qcs, kv, qc, qs, lens, stage, eb, e, gws, total, acc, dkv, gqs, gq, rd,
    sd, gbs, r2a, r2b, s2a, s2b, r3a, r3b, s3, rk, loc, out_sems, in_sems,
):
    row, key, a, x, z, y, core = place()
    rows_dev, block, feature = q.shape
    length = bias.shape[2]
    dim = feature // NX
    factor = 1.0 / math.sqrt(dim)
    sems = [(out_sems.at[n], in_sems.at[n]) for n in range(EXCHANGES)]
    m0, m1a, m1b, mkv, mqc, mswap, n3a, n3b, n4, nkv, ngq, nswap, mlen = sems[:13]
    m2, n2 = sems[13:17], sems[17:21]
    other = row_of(z, y, 1 - core)
    half = lax.div(x, 2)
    side = lax.rem(x, 2)
    here = half == core

    def y_peer(s):
        return (row_of(z, lax.rem(y + s, NY), core), key)

    def z_peer(s):
        return (row_of(lax.rem(z + s, nz), y, core), key)

    ys, zs, xs = far_first(NY), far_first(nz), far_first(NX)
    barrier = pltpu.get_barrier_semaphore()
    peers = [(row, lax.rem(key + s, NA * NX)) for s in range(1, NA * NX)]
    peers += [(other, a * NX + lax.rem(x + s, NX)) for s in range(NX)]
    peers += [z_peer(s) for s in zs] + [y_peer(s) for s in ys]
    for peer in peers:
        pl.semaphore_signal(barrier, inc=1, device_id=peer, device_id_type=MESH)

    for h in range(NX):
        lines = bias[h].astype(F32)
        for j in range(2):
            for t in range(8):
                n = h * 16 + j * 8 + t
                stage[n : n + 1, :] = lines[j : j + 1, t * 128 : (t + 1) * 128]
    for h in range(NX):
        pieces[h] = stage[h * 16 : (h + 1) * 16, :].astype(BF)
    spots = lax.broadcasted_iota(jnp.int32, (8, 128), 0)
    known = jnp.zeros((8, 128), F32)
    for i in range(rows_dev):
        known = jnp.where(spots == i, lengths[i].astype(F32), known)
    lens[core] = known
    pl.semaphore_wait(barrier, len(peers))

    target = row_of(z, y, half)

    def heads(source, dest, sems):
        return [
            remote(
                source.at[lax.rem(x + s, NX)], dest, sems, (target, a * NX + lax.rem(x + s, NX))
            )
            for s in [2, 1, 3, 0]
        ]

    def take_some(sem, like):
        pl.when(here)(lambda: take(sem, like.at[0:3]))
        pl.when(jnp.logical_not(here))(lambda: take(sem, like))

    def launch(copies):
        start(copies[:-1])
        pl.when(jnp.logical_not(here))(copies[-1].start)

    first = heads(pieces, own.at[side, core], m0)
    launch(first)

    @pl.when(here)
    def _():
        own[side, core] = pieces[x]

    tell = start([remote(lens.at[core], lens.at[core], mlen, (other, key))])
    for part, source in enumerate((k, v)):
        for i in range(rows_dev):
            turned = source[i].T
            for h in range(NX):
                kvs[h, part, i] = turned[h * dim : (h + 1) * dim]
    others = []
    for s in (6, 2, 5, 7, 1, 3, 4):
        to = lax.rem(key + s, NA * NX)
        others.append(
            remote(
                kvs.at[lax.rem(to, NX)], kv.at[core, :, :, :, pl.ds(key * 128, 128)],
                mkv, (row, to),
            )
        )
    start(others)
    mine = start(
        [pltpu.make_async_copy(kvs.at[x], kv.at[core, :, :, :, pl.ds(key * 128, 128)], loc.at[0])]
    )

    for part, source in enumerate((q, c)):
        for i in range(rows_dev):
            lines = []
            for n in range(2 * nz):
                at = jnp.where(side == 1, (n % nz) * 2 + n // nz, n)
                lines.append(source[i, pl.ds(pl.multiple_of(at * 16, 16), 16)])
            turned = jnp.concatenate(lines, axis=0).T
            for h in range(NX):
                qcs[h, part, i] = turned[h * dim : (h + 1) * dim]

    asks = heads(qcs, qc.at[core, :, :, :, pl.ds(side * 128, 128)], mqc)
    launch(asks)
    keep = pltpu.make_async_copy(
        qcs.at[x], qc.at[core, :, :, :, pl.ds(side * 128, 128)], loc.at[1]
    )
    pl.when(here)(keep.start)

    take_some(m0[1], pieces)
    phase1a = start([remote(own.at[0], bg.at[0, z, y], m1a, z_peer(s)) for s in zs])
    phase1b = start([remote(own.at[1], bg.at[1, z, y], m1b, y_peer(s)) for s in ys])
    for b in range(2):
        bg[b, z, y] = own[b]
    phase2 = {}
    take(m1a[1], r3a)
    for n in range(2):
        piece = bg.at[0, n * nz // 2 : (n + 1) * nz // 2, y]
        phase2[n] = start(
            [remote(piece, piece, m2[n], y_peer(s)) for s in ys]
        )
    take(m1b[1], r3b)
    for n in range(2):
        piece = bg.at[1, z, n * NY // 2 : (n + 1) * NY // 2]
        phase2[2 + n] = start(
            [remote(piece, piece, m2[2 + n], z_peer(s)) for s in zs]
        )

    take(mkv[1], rk.at[0:7])
    mine[0].wait()
    swap = start([remote(kv.at[core], kv.at[core], mswap, (other, key))])
    take_some(mqc[1], qcs)
    pl.when(here)(keep.wait)
    lane = lax.broadcasted_iota(jnp.int32, (16, length), 1).astype(F32)
    line = lax.broadcasted_iota(jnp.int32, (16, length), 0)
    span = 2 * block
    part_rows = span // 4

    def early(n, carry):
        g, i = n // rows_dev, n % rows_dev
        scaled = qc[g, 0, i].astype(F32) * (factor * LOG2E)
        hi = scaled.astype(BF)
        rest = scaled - hi.astype(F32)
        mid = rest.astype(BF)
        low = (rest - mid.astype(F32)).astype(BF)
        ones = jnp.where(lax.broadcasted_iota(jnp.int32, (dim, span), 0) == 0, 1.0, 0.0).astype(BF)
        q3 = jnp.concatenate([hi, mid, low, ones], axis=0).T
        keys = kv[g, 0, i]
        valid = jnp.concatenate([lens[g, pl.ds(i, 1), :]] * (length // 128), axis=1)
        hidden = jnp.where((line == 0) & (lane >= valid), -1e30, 0.0).astype(BF)
        k3 = jnp.concatenate([keys, keys, keys, hidden, jnp.zeros_like(hidden)], axis=0)
        s = jnp.dot(q3, k3, preferred_element_type=F32)
        e[g, i] = jnp.exp2(s - jnp.max(s, axis=1, keepdims=True))
        for part in range(2):
            lines = qc[g, part, i].T
            for n in range(4):
                qs[n, g, part, i] = lines[n * part_rows : (n + 1) * part_rows].T
        gws[g, i] = jnp.dot(qc[g, 1, i].T, kv[g, 1, i], preferred_element_type=F32)
        return carry

    def early_rows(g):
        lax.fori_loop(g * rows_dev, (g + 1) * rows_dev, early, 0)

    early_rows(core)
    take(mswap[1], rd)
    take(mlen[1], lens.at[0])
    early_rows(1 - core)
    acc[...] = jnp.zeros_like(acc)
    total[...] = jnp.zeros_like(total)

    def chunks(n):
        if n < 2:
            return nz // 2, NY, lambda zz: (0, n * nz // 2 + zz, slice(None))
        return nz, NY // 2, lambda zz: (1, zz, slice((n - 2) * NY // 2, (n - 1) * NY // 2))

    def lay(n):
        count, wide, at = chunks(n)

        def part(zz, carry):
            stage[: wide * NC * 16] = (
                bg[at(zz)].astype(F32).reshape(wide * NC * 16, 128) * LOG2E
            )
            for g in range(wide * NC // 4):
                for t in range(8):
                    j0 = pl.multiple_of(n * part_rows + zz * (wide * NC * 2) + g * 8, 8)
                    eb[pl.ds(j0, 8), t * 128 : (t + 1) * 128] = jnp.exp2(
                        stage[pl.ds(g * 64 + t, 8, stride=8), :]
                    )
            return carry

        lax.fori_loop(0, count, part, 0)

    def late(n, g):
        rows = slice(n * part_rows, (n + 1) * part_rows)

        def one(i, carry):
            p = e[g, i, rows] * eb[rows]
            gw = gws[g, i, rows]
            inv = 1.0 / jnp.sum(p, axis=1, keepdims=True)
            w = p * inv
            grad = w * (gw - jnp.sum(p * gw, axis=1, keepdims=True) * inv)
            total[rows] += grad
            low = grad.astype(BF)
            gqs[n, g, i] = lax.dot_general(
                kv[g, 0, i], low, (((1,), (1,)), ((), ())), preferred_element_type=F32
            )
            acc[g, 0, i] += jnp.dot(qs[n, g, 0, i], low, preferred_element_type=F32)
            acc[g, 1, i] += jnp.dot(qs[n, g, 1, i], w.astype(BF), preferred_element_type=F32)
            return carry

        lax.fori_loop(0, rows_dev, one, 0, unroll=4)

    def unlay(n):
        count, wide, at = chunks(n)

        def part(zz, carry):
            for g in range(wide * NC // 4):
                for t in range(8):
                    j0 = pl.multiple_of(n * part_rows + zz * (wide * NC * 2) + g * 8, 8)
                    stage[pl.ds(g * 64 + t, 8, stride=8), :] = total[
                        pl.ds(j0, 8), t * 128 : (t + 1) * 128
                    ]
            gbs[at(zz)] = stage[: wide * NC * 16].reshape(wide, NC, 16, 128).astype(BF)
            return carry

        lax.fori_loop(0, count, part, 0)

    order = (0, 2, 3, 1)
    sum2 = {}
    for turn, n in enumerate(order):
        take(m2[n][1], r2a.at[0] if n < 2 else r2b.at[0])
        lay(n)
        late(n, 1 - core)
        if turn == 3:
            for i in range(rows_dev):
                dkv[1 - core, 0, i] = (acc[1 - core, 0, i] * factor).astype(BF)
                dkv[1 - core, 1, i] = acc[1 - core, 1, i].astype(BF)
            give = start([remote(dkv.at[1 - core], rd, nswap, (other, key))])
        late(n, core)
        unlay(n)
        if n < 2:
            sum2[n] = [
                remote(
                    gbs.at[0, n * nz // 2 : (n + 1) * nz // 2, lax.rem(y + s, NY)],
                    r2a.at[n, s - 1], n2[n], y_peer(s),
                )
                for s in ys
            ]
        else:
            sum2[n] = [
                remote(
                    gbs.at[1, lax.rem(z + s, nz), (n - 2) * NY // 2 : (n - 1) * NY // 2],
                    r2b.at[n - 2, s - 1], n2[n], z_peer(s),
                )
                for s in zs
            ]
        start(sum2[n])
    for g in range(NC):
        for i in range(rows_dev):
            gq[g, i] = (
                jnp.concatenate([gqs[n, g, i] for n in range(4)], axis=1) * factor
            ).astype(BF)

    backs = []
    for b in range(2):
        for g in range(NC):
            away = jnp.logical_not((x == core * 2 + b) & (core == g))
            piece = gq.at[g, :, :, b * 128 : (b + 1) * 128]
            owner = (row_of(z, y, g), a * NX + core * 2 + b)
            cp = remote(piece, rq.at[x], ngq, owner)
            pl.when(away)(cp.start)
            keep = pltpu.make_async_copy(piece, rq.at[x], loc.at[2])
            pl.when(jnp.logical_not(away))(keep.start)
            backs.append((away, keep))
    take(nswap[1], rd)
    for i in range(rows_dev):
        sd[0, i] = (acc[core, 0, i] * factor + rd[0, i].astype(F32)).astype(BF)
        sd[1, i] = (acc[core, 1, i] + rd[1, i].astype(F32)).astype(BF)
    outs = []
    for s in (6, 2, 5, 7, 1, 3, 4):
        to = lax.rem(key + s, NA * NX)
        outs.append(
            remote(
                sd.at[:, :, :, pl.ds(to * 128, 128)], rk.at[key], nkv, (row, to)
            )
        )
    start(outs)
    held = start(
        [pltpu.make_async_copy(sd.at[:, :, :, pl.ds(key * 128, 128)], rk.at[key], loc.at[3])]
    )

    take(n2[2][1], r2b.at[0])
    take(n2[3][1], r2b.at[1])
    for n in range(2):
        part = gbs[1, z, n * NY // 2 : (n + 1) * NY // 2].astype(F32)
        for s in range(nz - 1):
            part += r2b[n, s].astype(F32)
        s2b[n * NY // 2 : (n + 1) * NY // 2] = part.astype(BF)
    sum3b = start(
        [
            remote(s2b.at[lax.rem(y + s, NY)], r3b.at[s - 1], n3b, y_peer(s))
            for s in ys
        ]
    )
    take(n2[0][1], r2a.at[0])
    take(n2[1][1], r2a.at[1])
    for n in range(2):
        part = gbs[0, n * nz // 2 : (n + 1) * nz // 2, y].astype(F32)
        for s in range(NY - 1):
            part += r2a[n, s].astype(F32)
        s2a[n * nz // 2 : (n + 1) * nz // 2] = part.astype(BF)
    sum3a = start(
        [
            remote(s2a.at[lax.rem(z + s, nz)], r3a.at[s - 1], n3a, z_peer(s))
            for s in zs
        ]
    )
    take(n3a[1], r3a)
    part = s2a[z].astype(F32)
    for s in range(nz - 1):
        part += r3a[s].astype(F32)
    s3[0] = part
    take(n3b[1], r3b)
    part = s2b[y].astype(F32)
    for s in range(NY - 1):
        part += r3b[s].astype(F32)
    s3[1] = part
    for b in range(2):
        for g in range(NC):
            away = jnp.logical_not((x == core * 2 + b) & (core == g))
            owner = (row_of(z, y, g), a * NX + core * 2 + b)
            cp = remote(s3.at[b, g], r4.at[x], n4, owner)
            pl.when(away)(cp.start)

    @pl.when(here)
    def _():
        r4[x] = s3[side, core]

    take(nkv[1], rk.at[0:7])
    held[0].wait()
    for i in range(rows_dev):
        for part in range(2):
            for h in range(NX):
                ks[part, i, h * dim : (h + 1) * dim] = (
                    rk[h, part, i].astype(F32) + rk[NX + h, part, i].astype(F32)
                ).astype(BF)
    for away, keep in backs:
        pl.when(jnp.logical_not(away))(keep.wait)
    take_some(ngq[1], rq)
    take_some(n4[1], r4)
    take_some(m0[0], pieces)
    take_some(mqc[0], qcs)
    take_some(ngq[0], rq)
    take_some(n4[0], r4)
    for group, like in (
        (m1a, r3a), (m1b, r3b), (n3a, r3a), (n3b, r3b), (mkv, rk.at[0:7]), (nkv, rk.at[0:7]),
        (mswap, rd), (nswap, rd), (mlen, lens.at[0]),
    ):
        take(group[0], like)
    for group in (m2, n2):
        for n in range(4):
            take(group[n][0], r2a.at[0] if n < 2 else r2b.at[0])


def finish(nz, rq, ks, r4, oq, ok, ov, ob, held):
    odd = lax.rem(lax.axis_index("key"), 2)
    for i in range(oq.shape[0]):
        held[...] = jnp.concatenate([rq[h, i] for h in range(NX)], axis=0).T
        for n in range(2 * nz):
            at = jnp.where(odd == 1, (n % 2) * nz + n // 2, n)
            oq[i, n * 16 : (n + 1) * 16] = held[pl.ds(pl.multiple_of(at * 16, 16), 16)]
        ok[i] = ks[0, i].T
        ov[i] = ks[1, i].T
    for h in range(NX):
        for j in range(2):
            for t in range(8):
                n = j * 8 + t
                ob[h, j : j + 1, t * 128 : (t + 1) * 128] = r4[h, n : n + 1, :]


def dma(*shape):
    return pltpu.SemaphoreType.DMA(shape)


def per_device(queries, keys_in, values, cotangent, pair_bias, key_lengths):
    rows_dev, block, feature = queries.shape
    heads, owned, length = pair_bias.shape
    dim = feature // heads
    nz = lax.axis_size("row") // (NY * NC)
    tile = (owned * length // 128, 128)
    span = 2 * block
    vmem = pl.BlockSpec(memory_space=VM)
    kind = jax.ShapeDtypeStruct(queries.shape, BF)
    scratch = [
        VM((NX,) + tile, BF),
        VM((2, NC) + tile, BF),
        VM((2, nz, NY, NC) + tile, BF),
        VM((NX, 2, rows_dev, dim, block), BF),
        VM((NX, 2, rows_dev, dim, block), BF),
        VM((NC, 2, rows_dev, dim, length), BF),
        VM((NC, 2, rows_dev, dim, span), BF),
        VM((4, NC, 2, rows_dev, dim, span // 4), BF),
        VM((NC, 8, 128), F32),
        VM((NY * NC * tile[0], 128), F32),
        VM((span, length), F32),
        VM((NC, rows_dev, span, length), F32),
        VM((NC, rows_dev, span, length), F32),
        VM((span, length), F32),
        VM((NC, 2, rows_dev, dim, length), F32),
        VM((NC, 2, rows_dev, dim, length), BF),
        VM((4, NC, rows_dev, dim, span // 4), F32),
        VM((NC, rows_dev, dim, span), BF),
        VM((2, rows_dev, dim, length), BF),
        VM((2, rows_dev, dim, length), BF),
        VM((2, nz, NY, NC) + tile, BF),
        VM((2, NY - 1, nz // 2, NC) + tile, BF),
        VM((2, nz - 1, NY // 2, NC) + tile, BF),
        VM((nz, NC) + tile, BF),
        VM((NY, NC) + tile, BF),
        VM((nz - 1, NC) + tile, BF),
        VM((NY - 1, NC) + tile, BF),
        VM((2, NC) + tile, F32),
        VM((NA * NX, 2, rows_dev, dim, block), BF),
        dma(4),
        dma(EXCHANGES),
        dma(EXCHANGES),
    ]
    passed = (
        jax.ShapeDtypeStruct((NX, rows_dev, dim, block), BF),
        jax.ShapeDtypeStruct((2, rows_dev, feature, block), BF),
        jax.ShapeDtypeStruct((heads,) + tile, F32),
    )
    parts = pl.pallas_call(
        lambda *refs: kernel(nz, *refs),
        out_shape=passed,
        in_specs=[pl.BlockSpec(memory_space=pltpu.SMEM)] + [vmem] * 5,
        out_specs=(vmem,) * 3,
        scratch_shapes=scratch,
        compiler_params=pltpu.CompilerParams(
            collective_id=0, has_side_effects=True, vmem_limit_bytes=60 * 1024 * 1024
        ),
        name="attention_grad",
    )(key_lengths, queries, keys_in, values, cotangent, pair_bias)
    return pl.pallas_call(
        lambda *refs: finish(nz, *refs),
        out_shape=(kind, kind, kind, jax.ShapeDtypeStruct(pair_bias.shape, F32)),
        in_specs=[vmem] * 3,
        out_specs=(vmem,) * 4,
        scratch_shapes=[VM((block, feature), BF)],
        compiler_params=pltpu.CompilerParams(vmem_limit_bytes=60 * 1024 * 1024),
        name="finish",
    )(*parts)


def solution(mesh):
    wide = P("row", "key", None)
    bias = P(None, ("key", "row"), None)
    return jax.shard_map(
        per_device,
        mesh=mesh,
        in_specs=(wide, wide, wide, wide, bias, P("row")),
        out_specs=(wide, wide, wide, bias),
        check_vma=False,
    )
```

```python
import math

import jax
import jax.numpy as jnp
from jax import lax
from jax.experimental import pallas as pl
from jax.experimental.pallas import tpu as pltpu
from jax.sharding import PartitionSpec as P

MESH = pl.DeviceIdType.MESH
VM = pltpu.VMEM
BF = jnp.bfloat16
F32 = jnp.float32
NX, NA = 4, 2
NY, NC = 8, 2
LOG2E = 1.4426950408889634
EXCHANGES = 21


def place():
    row, key = lax.axis_index("row"), lax.axis_index("key")
    return (
        row,
        key,
        lax.div(key, NX),
        lax.rem(key, NX),
        lax.div(row, NY * NC),
        lax.rem(lax.div(row, NC), NY),
        lax.rem(row, NC),
    )


def row_of(z, y, core):
    return (z * NY + y) * NC + core


def remote(src, dst, sems, peer):
    return pltpu.make_async_remote_copy(
        src_ref=src,
        dst_ref=dst,
        send_sem=sems[0],
        recv_sem=sems[1],
        device_id=peer,
        device_id_type=MESH,
    )


def take(sem, like):
    pltpu.make_async_copy(like, like, sem).wait()


def start(copies):
    for cp in copies:
        cp.start()
    return copies


def far_first(n):
    return sorted(range(1, n), key=lambda s: -min(s, n - s))


def kernel(
    nz, lengths, q_in, k_in, v_in, c_in, bias, oq, ok, ov, r4,
    q, k, v, c, rq, done,
    pieces, own, bg, kvs, qcs, kv, qc, qs, lens, stage, eb, e, gws, total, acc, dkv, gqs, gq, rd,
    sd, gbs, r2a, r2b, s2a, s2b, r3a, r3b, r5, rk, loc, out_sems, in_sems,
):
    row, key, a, x, z, y, core = place()
    rows_dev, block, feature = q.shape
    length = bias.shape[2]
    dim = feature // NX
    factor = 1.0 / math.sqrt(dim)
    sems = [(out_sems.at[n], in_sems.at[n]) for n in range(EXCHANGES)]
    m0, m1a, m1b, mkv, mqc, mswap, n3a, n3b, n4, nkv, ngq, nswap, mlen = sems[:13]
    m2, n2 = sems[13:17], sems[17:21]
    other = row_of(z, y, 1 - core)
    half = lax.div(x, 2)
    side = lax.rem(x, 2)
    here = half == core

    def y_peer(s):
        return (row_of(z, lax.rem(y + s, NY), core), key)

    def z_peer(s):
        return (row_of(lax.rem(z + s, nz), y, core), key)

    loads = start(
        [
            pltpu.make_async_copy(there, held, loc.at[4 + n])
            for n, (there, held) in enumerate(((k_in, k), (v_in, v), (q_in, q), (c_in, c)))
        ]
    )
    ys, zs, xs = far_first(NY), far_first(nz), far_first(NX)
    barrier = pltpu.get_barrier_semaphore()
    peers = [(row, lax.rem(key + s, NA * NX)) for s in range(1, NA * NX)]
    peers += [(other, a * NX + lax.rem(x + s, NX)) for s in range(NX)]
    peers += [z_peer(s) for s in zs] + [y_peer(s) for s in ys]
    for peer in peers:
        pl.semaphore_signal(barrier, inc=1, device_id=peer, device_id_type=MESH)

    def gatherers(even):
        found = []
        for s in zs + [0] if even else ys + [0]:
            at = row_of(lax.rem(z + s, nz), y, half) if even else row_of(z, lax.rem(y + s, NY), half)
            for t in [2, 1, 3, 0]:
                to = lax.rem(x + t, NX)
                found.append((s == 0 and t == 0, to, (at, a * NX + to)))
        return found

    def owners(even):
        found = []
        for s in zs + [0] if even else ys + [0]:
            for g in range(NC):
                if even:
                    at, zy = row_of(lax.rem(z + s, nz), y, g), lax.rem(z + s, nz)
                else:
                    at, zy = row_of(z, lax.rem(y + s, NY), g), lax.rem(y + s, NY)
                same = (core == g) & here & (side == (0 if even else 1))
                found.append((s == 0, same, zy, g, (at, a * NX + core * 2 + (0 if even else 1))))
        return found

    def greet(peer):
        pl.semaphore_signal(barrier, inc=1, device_id=peer, device_id_type=MESH)

    for even in (True, False):

        @pl.when(side == (0 if even else 1))
        def _():
            for maybe, _, peer in gatherers(even):
                if maybe:
                    pl.when(jnp.logical_not(here))(lambda: greet(peer))
                else:
                    greet(peer)

        for maybe, same, _, _, peer in owners(even):
            if maybe:
                pl.when(jnp.logical_not(same))(lambda: greet(peer))
            else:
                greet(peer)

    for h in range(NX):
        lines = bias[h].astype(F32)
        for j in range(2):
            for t in range(8):
                n = h * 16 + j * 8 + t
                stage[n : n + 1, :] = lines[j : j + 1, t * 128 : (t + 1) * 128]
    for h in range(NX):
        pieces[h] = stage[h * 16 : (h + 1) * 16, :].astype(BF)
    spots = lax.broadcasted_iota(jnp.int32, (8, 128), 0)
    known = jnp.zeros((8, 128), F32)
    for i in range(rows_dev):
        known = jnp.where(spots == i, lengths[i].astype(F32), known)
    lens[core] = known
    several = jnp.where(side == 0, NX * nz, NX * NY) + NC * (nz + NY)
    pl.semaphore_wait(barrier, len(peers) + several - jnp.where(here, 2, 0))

    target = row_of(z, y, half)

    def heads(source, dest, sems):
        return [
            remote(
                source.at[lax.rem(x + s, NX)], dest, sems, (target, a * NX + lax.rem(x + s, NX))
            )
            for s in [2, 1, 3, 0]
        ]

    def take_some(sem, like):
        pl.when(here)(lambda: take(sem, like.at[0:3]))
        pl.when(jnp.logical_not(here))(lambda: take(sem, like))

    def launch(copies):
        start(copies[:-1])
        pl.when(jnp.logical_not(here))(copies[-1].start)

    first = heads(pieces, own.at[side, core], m0)
    launch(first)

    @pl.when(here)
    def _():
        own[side, core] = pieces[x]

    tell = start([remote(lens.at[core], lens.at[core], mlen, (other, key))])
    loads[0].wait()
    loads[1].wait()
    for part, source in enumerate((k, v)):
        for i in range(rows_dev):
            turned = source[i].T
            for h in range(NX):
                kvs[h, part, i] = turned[h * dim : (h + 1) * dim]
    others = []
    for s in (6, 2, 5, 7, 1, 3, 4):
        to = lax.rem(key + s, NA * NX)
        others.append(
            remote(
                kvs.at[lax.rem(to, NX)], kv.at[core, :, :, :, pl.ds(key * 128, 128)],
                mkv, (row, to),
            )
        )
    start(others)
    mine = start(
        [pltpu.make_async_copy(kvs.at[x], kv.at[core, :, :, :, pl.ds(key * 128, 128)], loc.at[0])]
    )

    loads[2].wait()
    loads[3].wait()
    for part, source in enumerate((q, c)):
        for i in range(rows_dev):
            lines = []
            for n in range(2 * nz):
                at = jnp.where(side == 1, (n % nz) * 2 + n // nz, n)
                lines.append(source[i, pl.ds(pl.multiple_of(at * 16, 16), 16)])
            turned = jnp.concatenate(lines, axis=0).T
            for h in range(NX):
                qcs[h, part, i] = turned[h * dim : (h + 1) * dim]

    asks = heads(qcs, qc.at[core, :, :, :, pl.ds(side * 128, 128)], mqc)
    launch(asks)
    keep = pltpu.make_async_copy(
        qcs.at[x], qc.at[core, :, :, :, pl.ds(side * 128, 128)], loc.at[1]
    )
    pl.when(here)(keep.start)

    take_some(m0[1], pieces)
    phase1a = start([remote(own.at[0], bg.at[0, z, y], m1a, z_peer(s)) for s in zs])
    phase1b = start([remote(own.at[1], bg.at[1, z, y], m1b, y_peer(s)) for s in ys])
    for b in range(2):
        bg[b, z, y] = own[b]
    phase2 = {}
    take(m1a[1], r3a)
    for n in range(2):
        piece = bg.at[0, n * nz // 2 : (n + 1) * nz // 2, y]
        phase2[n] = start(
            [remote(piece, piece, m2[n], y_peer(s)) for s in ys]
        )
    take(m1b[1], r3b)
    for n in range(2):
        piece = bg.at[1, z, n * NY // 2 : (n + 1) * NY // 2]
        phase2[2 + n] = start(
            [remote(piece, piece, m2[2 + n], z_peer(s)) for s in zs]
        )

    take(mkv[1], rk.at[0:7])
    mine[0].wait()
    swap = start([remote(kv.at[core], kv.at[core], mswap, (other, key))])
    take_some(mqc[1], qcs)
    pl.when(here)(keep.wait)
    lane = lax.broadcasted_iota(jnp.int32, (16, length), 1).astype(F32)
    line = lax.broadcasted_iota(jnp.int32, (16, length), 0)
    span = 2 * block
    part_rows = span // 4

    def early(n, carry):
        g, i = n // rows_dev, n % rows_dev
        scaled = qc[g, 0, i].astype(F32) * (factor * LOG2E)
        hi = scaled.astype(BF)
        rest = scaled - hi.astype(F32)
        mid = rest.astype(BF)
        low = (rest - mid.astype(F32)).astype(BF)
        ones = jnp.where(lax.broadcasted_iota(jnp.int32, (dim, span), 0) == 0, 1.0, 0.0).astype(BF)
        q3 = jnp.concatenate([hi, mid, low, ones], axis=0).T
        keys = kv[g, 0, i]
        valid = jnp.concatenate([lens[g, pl.ds(i, 1), :]] * (length // 128), axis=1)
        hidden = jnp.where((line == 0) & (lane >= valid), -1e30, 0.0).astype(BF)
        k3 = jnp.concatenate([keys, keys, keys, hidden, jnp.zeros_like(hidden)], axis=0)
        s = jnp.dot(q3, k3, preferred_element_type=F32)
        e[g, i] = jnp.exp2(s - jnp.max(s, axis=1, keepdims=True))
        for part in range(2):
            lines = qc[g, part, i].T
            for n in range(4):
                qs[n, g, part, i] = lines[n * part_rows : (n + 1) * part_rows].T
        gws[g, i] = jnp.dot(qc[g, 1, i].T, kv[g, 1, i], preferred_element_type=F32)
        return carry

    def early_rows(g):
        lax.fori_loop(g * rows_dev, (g + 1) * rows_dev, early, 0)

    early_rows(core)
    take(mswap[1], rd)
    take(mlen[1], lens.at[0])
    early_rows(1 - core)
    acc[...] = jnp.zeros_like(acc)
    total[...] = jnp.zeros_like(total)

    def chunks(n):
        if n < 2:
            return nz // 2, NY, lambda zz: (0, n * nz // 2 + zz, slice(None))
        return nz, NY // 2, lambda zz: (1, zz, slice((n - 2) * NY // 2, (n - 1) * NY // 2))

    def lay(n):
        count, wide, at = chunks(n)

        def part(zz, carry):
            stage[: wide * NC * 16] = (
                bg[at(zz)].astype(F32).reshape(wide * NC * 16, 128) * LOG2E
            )
            for g in range(wide * NC // 4):
                for t in range(8):
                    j0 = pl.multiple_of(n * part_rows + zz * (wide * NC * 2) + g * 8, 8)
                    eb[pl.ds(j0, 8), t * 128 : (t + 1) * 128] = jnp.exp2(
                        stage[pl.ds(g * 64 + t, 8, stride=8), :]
                    )
            return carry

        lax.fori_loop(0, count, part, 0)

    def late(n, g):
        rows = slice(n * part_rows, (n + 1) * part_rows)

        def one(i, carry):
            p = e[g, i, rows] * eb[rows]
            gw = gws[g, i, rows]
            inv = 1.0 / jnp.sum(p, axis=1, keepdims=True)
            w = p * inv
            grad = w * (gw - jnp.sum(p * gw, axis=1, keepdims=True) * inv)
            total[rows] += grad
            low = grad.astype(BF)
            gqs[n, g, i] = lax.dot_general(
                kv[g, 0, i], low, (((1,), (1,)), ((), ())), preferred_element_type=F32
            )
            acc[g, 0, i] += jnp.dot(qs[n, g, 0, i], low, preferred_element_type=F32)
            acc[g, 1, i] += jnp.dot(qs[n, g, 1, i], w.astype(BF), preferred_element_type=F32)
            return carry

        lax.fori_loop(0, rows_dev, one, 0, unroll=4)

    def unlay(n):
        count, wide, at = chunks(n)

        def part(zz, carry):
            for g in range(wide * NC // 4):
                for t in range(8):
                    j0 = pl.multiple_of(n * part_rows + zz * (wide * NC * 2) + g * 8, 8)
                    stage[pl.ds(g * 64 + t, 8, stride=8), :] = total[
                        pl.ds(j0, 8), t * 128 : (t + 1) * 128
                    ]
            gbs[at(zz)] = stage[: wide * NC * 16].reshape(wide, NC, 16, 128).astype(BF)
            return carry

        lax.fori_loop(0, count, part, 0)

    order = (0, 2, 3, 1)
    sum2 = {}
    for turn, n in enumerate(order):
        take(m2[n][1], r2a.at[0] if n < 2 else r2b.at[0])
        lay(n)
        late(n, 1 - core)
        if turn == 3:
            for i in range(rows_dev):
                dkv[1 - core, 0, i] = (acc[1 - core, 0, i] * factor).astype(BF)
                dkv[1 - core, 1, i] = acc[1 - core, 1, i].astype(BF)
            give = start([remote(dkv.at[1 - core], rd, nswap, (other, key))])
        late(n, core)
        unlay(n)
        if n < 2:
            sum2[n] = [
                remote(
                    gbs.at[0, n * nz // 2 : (n + 1) * nz // 2, lax.rem(y + s, NY)],
                    r2a.at[n, s - 1], n2[n], y_peer(s),
                )
                for s in ys
            ]
        else:
            sum2[n] = [
                remote(
                    gbs.at[1, lax.rem(z + s, nz), (n - 2) * NY // 2 : (n - 1) * NY // 2],
                    r2b.at[n - 2, s - 1], n2[n], z_peer(s),
                )
                for s in zs
            ]
        start(sum2[n])
    for g in range(NC):
        for i in range(rows_dev):
            gq[g, i] = (
                jnp.concatenate([gqs[n, g, i] for n in range(4)], axis=1) * factor
            ).astype(BF)

    backs = []
    for b in range(2):
        for g in range(NC):
            away = jnp.logical_not((x == core * 2 + b) & (core == g))
            piece = gq.at[g, :, :, b * 128 : (b + 1) * 128]
            owner = (row_of(z, y, g), a * NX + core * 2 + b)
            cp = remote(piece, rq.at[x], ngq, owner)
            pl.when(away)(cp.start)
            keep = pltpu.make_async_copy(piece, rq.at[x], loc.at[2])
            pl.when(jnp.logical_not(away))(keep.start)
            backs.append((away, keep))
    take(nswap[1], rd)
    for i in range(rows_dev):
        sd[0, i] = (acc[core, 0, i] * factor + rd[0, i].astype(F32)).astype(BF)
        sd[1, i] = (acc[core, 1, i] + rd[1, i].astype(F32)).astype(BF)
    outs = []
    for s in (6, 2, 5, 7, 1, 3, 4):
        to = lax.rem(key + s, NA * NX)
        outs.append(
            remote(
                sd.at[:, :, :, pl.ds(to * 128, 128)], rk.at[key], nkv, (row, to)
            )
        )
    start(outs)
    held = start(
        [pltpu.make_async_copy(sd.at[:, :, :, pl.ds(key * 128, 128)], rk.at[key], loc.at[3])]
    )

    take(n2[2][1], r2b.at[0])
    take(n2[3][1], r2b.at[1])
    for n in range(2):
        part = gbs[1, z, n * NY // 2 : (n + 1) * NY // 2].astype(F32)
        for s in range(nz - 1):
            part += r2b[n, s].astype(F32)
        s2b[n * NY // 2 : (n + 1) * NY // 2] = part.astype(BF)
    def home(even, source):
        for maybe, same, zy, g, peer in owners(even):
            cp = remote(source.at[zy, g], r5.at[x * NY + (z if even else y)], n4, peer)
            if maybe:
                pl.when(jnp.logical_not(same))(cp.start)
            else:
                cp.start()

    home(False, s2b)
    take(n2[0][1], r2a.at[0])
    take(n2[1][1], r2a.at[1])
    for n in range(2):
        part = gbs[0, n * nz // 2 : (n + 1) * nz // 2, y].astype(F32)
        for s in range(NY - 1):
            part += r2a[n, s].astype(F32)
        s2a[n * nz // 2 : (n + 1) * nz // 2] = part.astype(BF)
    home(True, s2a)
    pl.when(here & (side == 0))(lambda: r5.__setitem__(x * NY + z, s2a[z, core]))
    pl.when(here & (side == 1))(lambda: r5.__setitem__(x * NY + y, s2b[y, core]))
    take(nkv[1], rk.at[0:7])
    held[0].wait()
    for i in range(rows_dev):
        for part in range(2):
            both = [
                rk[h, part, i].astype(F32) + rk[NX + h, part, i].astype(F32) for h in range(NX)
            ]
            done[1 + part, i] = jnp.concatenate(both, axis=0).astype(BF).T
    leaving = start([pltpu.make_async_copy(done.at[1], ok, loc.at[8]), pltpu.make_async_copy(done.at[2], ov, loc.at[9])])
    for away, keep in backs:
        pl.when(jnp.logical_not(away))(keep.wait)
    take_some(ngq[1], rq)
    for i in range(rows_dev):
        turned = jnp.concatenate([rq[h, i] for h in range(NX)], axis=0).T
        for n in range(2 * nz):
            at = jnp.where(side == 1, (n % nz) * 2 + n // nz, n)
            done[0, i, pl.ds(pl.multiple_of(at * 16, 16), 16)] = turned[n * 16 : (n + 1) * 16]
    leaving += start([pltpu.make_async_copy(done.at[0], oq, loc.at[10])])
    for even, count in ((True, nz), (False, NY)):

        @pl.when(side == (0 if even else 1))
        def _():
            pl.when(here)(lambda: take(n4[1], r5.at[0 : NX * count - 1]))
            pl.when(jnp.logical_not(here))(lambda: take(n4[1], r5.at[0 : NX * count]))
            for h in range(NX):
                part = r5[h * NY].astype(F32)
                for n in range(1, count):
                    part += r5[h * NY + n].astype(F32)
                r4[h] = part

    take_some(m0[0], pieces)
    take_some(mqc[0], qcs)
    take_some(ngq[0], rq)
    pl.when(here)(lambda: take(n4[0], r5.at[0:23]))
    pl.when(jnp.logical_not(here))(lambda: take(n4[0], r5.at[0:24]))
    for group, like in (
        (m1a, r3a), (m1b, r3b), (mkv, rk.at[0:7]), (nkv, rk.at[0:7]),
        (mswap, rd), (nswap, rd), (mlen, lens.at[0]),
    ):
        take(group[0], like)
    for group in (m2, n2):
        for n in range(4):
            take(group[n][0], r2a.at[0] if n < 2 else r2b.at[0])
    for cp in leaving:
        cp.wait()


def finish(q_in, k_in, v_in, r4, oq, ok, ov, ob):
    oq[...] = q_in[...]
    ok[...] = k_in[...]
    ov[...] = v_in[...]
    for h in range(NX):
        for j in range(2):
            for t in range(8):
                n = j * 8 + t
                ob[h, j : j + 1, t * 128 : (t + 1) * 128] = r4[h, n : n + 1, :]


def dma(*shape):
    return pltpu.SemaphoreType.DMA(shape)


def per_device(queries, keys_in, values, cotangent, pair_bias, key_lengths):
    rows_dev, block, feature = queries.shape
    heads, owned, length = pair_bias.shape
    dim = feature // heads
    nz = lax.axis_size("row") // (NY * NC)
    tile = (owned * length // 128, 128)
    span = 2 * block
    vmem = pl.BlockSpec(memory_space=VM)
    kind = jax.ShapeDtypeStruct(queries.shape, BF)
    scratch = [
        VM(queries.shape, BF),
        VM(queries.shape, BF),
        VM(queries.shape, BF),
        VM(queries.shape, BF),
        VM((NX, rows_dev, dim, block), BF),
        VM((3,) + queries.shape, BF),
        VM((NX,) + tile, BF),
        VM((2, NC) + tile, BF),
        VM((2, nz, NY, NC) + tile, BF),
        VM((NX, 2, rows_dev, dim, block), BF),
        VM((NX, 2, rows_dev, dim, block), BF),
        VM((NC, 2, rows_dev, dim, length), BF),
        VM((NC, 2, rows_dev, dim, span), BF),
        VM((4, NC, 2, rows_dev, dim, span // 4), BF),
        VM((NC, 8, 128), F32),
        VM((NY * NC * tile[0], 128), F32),
        VM((span, length), F32),
        VM((NC, rows_dev, span, length), F32),
        VM((NC, rows_dev, span, length), F32),
        VM((span, length), F32),
        VM((NC, 2, rows_dev, dim, length), F32),
        VM((NC, 2, rows_dev, dim, length), BF),
        VM((4, NC, rows_dev, dim, span // 4), F32),
        VM((NC, rows_dev, dim, span), BF),
        VM((2, rows_dev, dim, length), BF),
        VM((2, rows_dev, dim, length), BF),
        VM((2, nz, NY, NC) + tile, BF),
        VM((2, NY - 1, nz // 2, NC) + tile, BF),
        VM((2, nz - 1, NY // 2, NC) + tile, BF),
        VM((nz, NC) + tile, BF),
        VM((NY, NC) + tile, BF),
        VM((nz - 1, NC) + tile, BF),
        VM((NY - 1, NC) + tile, BF),
        VM((NX * NY,) + tile, BF),
        VM((NA * NX, 2, rows_dev, dim, block), BF),
        dma(11),
        dma(EXCHANGES),
        dma(EXCHANGES),
    ]
    passed = (kind, kind, kind, jax.ShapeDtypeStruct((heads,) + tile, F32))
    away = pl.BlockSpec(memory_space=pl.ANY)
    parts = pl.pallas_call(
        lambda *refs: kernel(nz, *refs),
        out_shape=passed,
        in_specs=[pl.BlockSpec(memory_space=pltpu.SMEM)] + [away] * 4 + [vmem],
        out_specs=(away,) * 3 + (vmem,),
        scratch_shapes=scratch,
        compiler_params=pltpu.CompilerParams(
            collective_id=0, has_side_effects=True, vmem_limit_bytes=60 * 1024 * 1024
        ),
        name="attention_grad",
    )(key_lengths, queries, keys_in, values, cotangent, pair_bias)
    return pl.pallas_call(
        finish,
        out_shape=(kind, kind, kind, jax.ShapeDtypeStruct(pair_bias.shape, F32)),
        in_specs=[vmem] * 4,
        out_specs=(vmem,) * 4,
        compiler_params=pltpu.CompilerParams(vmem_limit_bytes=60 * 1024 * 1024),
        name="finish",
    )(*parts)


def solution(mesh):
    wide = P("row", "key", None)
    bias = P(None, ("key", "row"), None)
    return jax.shard_map(
        per_device,
        mesh=mesh,
        in_specs=(wide, wide, wide, wide, bias, P("row")),
        out_specs=(wide, wide, wide, bias),
        check_vma=False,
    )
```

```python
import math

import jax
import jax.numpy as jnp
from jax import lax
from jax.experimental import pallas as pl
from jax.experimental.pallas import tpu as pltpu
from jax.sharding import PartitionSpec as P

MESH = pl.DeviceIdType.MESH
VM = pltpu.VMEM
BF = jnp.bfloat16
F32 = jnp.float32
NX, NA = 4, 2
NY, NC = 8, 2
LOG2E = 1.4426950408889634
EXCHANGES = 21


def place():
    row, key = lax.axis_index("row"), lax.axis_index("key")
    return (
        row,
        key,
        lax.div(key, NX),
        lax.rem(key, NX),
        lax.div(row, NY * NC),
        lax.rem(lax.div(row, NC), NY),
        lax.rem(row, NC),
    )


def row_of(z, y, core):
    return (z * NY + y) * NC + core


def remote(src, dst, sems, peer):
    return pltpu.make_async_remote_copy(
        src_ref=src,
        dst_ref=dst,
        send_sem=sems[0],
        recv_sem=sems[1],
        device_id=peer,
        device_id_type=MESH,
    )


def take(sem, like):
    pltpu.make_async_copy(like, like, sem).wait()


def start(copies):
    for cp in copies:
        cp.start()
    return copies


def far_first(n):
    return sorted(range(1, n), key=lambda s: -min(s, n - s))


def kernel(
    nz, lengths, q_in, k_in, v_in, c_in, bias, oq, ok, ov, r4,
    q, k, v, c, rq, done,
    pieces, own, bg, kvs, qcs, kv, qc, qs, lens, stage, eb, e, gws, total, acc, dkv, gqs, gq, rd,
    sd, gbs, r2a, r2b, s2a, s2b, r3a, r3b, r5, rk, loc, out_sems, in_sems,
):
    row, key, a, x, z, y, core = place()
    rows_dev, block, feature = q.shape
    length = bias.shape[2]
    dim = feature // NX
    factor = 1.0 / math.sqrt(dim)
    sems = [(out_sems.at[n], in_sems.at[n]) for n in range(EXCHANGES)]
    m0, m1a, m1b, mkv, mqc, mswap, n3a, n3b, n4, nkv, ngq, nswap, mlen = sems[:13]
    m2, n2 = sems[13:17], sems[17:21]
    other = row_of(z, y, 1 - core)
    half = lax.div(x, 2)
    side = lax.rem(x, 2)
    here = half == core

    def y_peer(s):
        return (row_of(z, lax.rem(y + s, NY), core), key)

    def z_peer(s):
        return (row_of(lax.rem(z + s, nz), y, core), key)

    loads = start(
        [
            pltpu.make_async_copy(there, held, loc.at[4 + n])
            for n, (there, held) in enumerate(((k_in, k), (v_in, v), (q_in, q), (c_in, c)))
        ]
    )
    ys, zs, xs = far_first(NY), far_first(nz), far_first(NX)
    barrier = pltpu.get_barrier_semaphore()
    peers = [(row, lax.rem(key + s, NA * NX)) for s in range(1, NA * NX)]
    peers += [(other, a * NX + lax.rem(x + s, NX)) for s in range(NX)]
    peers += [z_peer(s) for s in zs] + [y_peer(s) for s in ys]
    for peer in peers:
        pl.semaphore_signal(barrier, inc=1, device_id=peer, device_id_type=MESH)

    def gatherers(even):
        found = []
        for s in zs + [0] if even else ys + [0]:
            at = row_of(lax.rem(z + s, nz), y, half) if even else row_of(z, lax.rem(y + s, NY), half)
            for t in [2, 1, 3, 0]:
                to = lax.rem(x + t, NX)
                found.append((s == 0 and t == 0, to, (at, a * NX + to)))
        return found

    def owners(even):
        found = []
        for s in zs + [0] if even else ys + [0]:
            for g in range(NC):
                if even:
                    at, zy = row_of(lax.rem(z + s, nz), y, g), lax.rem(z + s, nz)
                else:
                    at, zy = row_of(z, lax.rem(y + s, NY), g), lax.rem(y + s, NY)
                same = (core == g) & here & (side == (0 if even else 1))
                found.append((s == 0, same, zy, g, (at, a * NX + core * 2 + (0 if even else 1))))
        return found

    def greet(peer):
        pl.semaphore_signal(barrier, inc=1, device_id=peer, device_id_type=MESH)

    for even in (True, False):

        @pl.when(side == (0 if even else 1))
        def _():
            for maybe, _, peer in gatherers(even):
                if maybe:
                    pl.when(jnp.logical_not(here))(lambda: greet(peer))
                else:
                    greet(peer)


    for h in range(NX):
        lines = bias[h].astype(F32)
        for j in range(2):
            for t in range(8):
                n = h * 16 + j * 8 + t
                stage[n : n + 1, :] = lines[j : j + 1, t * 128 : (t + 1) * 128]
    for h in range(NX):
        pieces[h] = stage[h * 16 : (h + 1) * 16, :].astype(BF)
    spots = lax.broadcasted_iota(jnp.int32, (8, 128), 0)
    known = jnp.zeros((8, 128), F32)
    for i in range(rows_dev):
        known = jnp.where(spots == i, lengths[i].astype(F32), known)
    lens[core] = known
    pl.semaphore_wait(barrier, len(peers) + NC * (nz + NY) - jnp.where(here, 1, 0))

    target = row_of(z, y, half)

    def heads(source, dest, sems):
        return [
            remote(
                source.at[lax.rem(x + s, NX)], dest, sems, (target, a * NX + lax.rem(x + s, NX))
            )
            for s in [2, 1, 3, 0]
        ]

    def take_some(sem, like):
        pl.when(here)(lambda: take(sem, like.at[0:3]))
        pl.when(jnp.logical_not(here))(lambda: take(sem, like))

    def launch(copies):
        start(copies[:-1])
        pl.when(jnp.logical_not(here))(copies[-1].start)

    first = heads(pieces, own.at[side, core], m0)
    launch(first)

    @pl.when(here)
    def _():
        own[side, core] = pieces[x]

    tell = start([remote(lens.at[core], lens.at[core], mlen, (other, key))])
    loads[0].wait()
    loads[1].wait()
    for part, source in enumerate((k, v)):
        for i in range(rows_dev):
            turned = source[i].T
            for h in range(NX):
                kvs[h, part, i] = turned[h * dim : (h + 1) * dim]
    others = []
    for s in (6, 2, 5, 7, 1, 3, 4):
        to = lax.rem(key + s, NA * NX)
        others.append(
            remote(
                kvs.at[lax.rem(to, NX)], kv.at[core, :, :, :, pl.ds(key * 128, 128)],
                mkv, (row, to),
            )
        )
    start(others)
    mine = start(
        [pltpu.make_async_copy(kvs.at[x], kv.at[core, :, :, :, pl.ds(key * 128, 128)], loc.at[0])]
    )

    loads[2].wait()
    loads[3].wait()
    for part, source in enumerate((q, c)):
        for i in range(rows_dev):
            lines = []
            for n in range(2 * nz):
                at = jnp.where(side == 1, (n % nz) * 2 + n // nz, n)
                lines.append(source[i, pl.ds(pl.multiple_of(at * 16, 16), 16)])
            turned = jnp.concatenate(lines, axis=0).T
            for h in range(NX):
                qcs[h, part, i] = turned[h * dim : (h + 1) * dim]

    asks = heads(qcs, qc.at[core, :, :, :, pl.ds(side * 128, 128)], mqc)
    launch(asks)
    keep = pltpu.make_async_copy(
        qcs.at[x], qc.at[core, :, :, :, pl.ds(side * 128, 128)], loc.at[1]
    )
    pl.when(here)(keep.start)

    take_some(m0[1], pieces)
    phase1a = start([remote(own.at[0], bg.at[0, z, y], m1a, z_peer(s)) for s in zs])
    phase1b = start([remote(own.at[1], bg.at[1, z, y], m1b, y_peer(s)) for s in ys])
    for b in range(2):
        bg[b, z, y] = own[b]
    phase2 = {}
    take(m1a[1], r3a)
    for n in range(2):
        piece = bg.at[0, n * nz // 2 : (n + 1) * nz // 2, y]
        phase2[n] = start(
            [remote(piece, piece, m2[n], y_peer(s)) for s in ys]
        )
    take(m1b[1], r3b)
    for n in range(2):
        piece = bg.at[1, z, n * NY // 2 : (n + 1) * NY // 2]
        phase2[2 + n] = start(
            [remote(piece, piece, m2[2 + n], z_peer(s)) for s in zs]
        )

    take(mkv[1], rk.at[0:7])
    mine[0].wait()
    swap = start([remote(kv.at[core], kv.at[core], mswap, (other, key))])
    take_some(mqc[1], qcs)
    pl.when(here)(keep.wait)
    lane = lax.broadcasted_iota(jnp.int32, (16, length), 1).astype(F32)
    line = lax.broadcasted_iota(jnp.int32, (16, length), 0)
    span = 2 * block
    part_rows = span // 4

    def early(n, carry):
        g, i = n // rows_dev, n % rows_dev
        scaled = qc[g, 0, i].astype(F32) * (factor * LOG2E)
        hi = scaled.astype(BF)
        rest = scaled - hi.astype(F32)
        mid = rest.astype(BF)
        low = (rest - mid.astype(F32)).astype(BF)
        ones = jnp.where(lax.broadcasted_iota(jnp.int32, (dim, span), 0) == 0, 1.0, 0.0).astype(BF)
        q3 = jnp.concatenate([hi, mid, low, ones], axis=0).T
        keys = kv[g, 0, i]
        valid = jnp.concatenate([lens[g, pl.ds(i, 1), :]] * (length // 128), axis=1)
        hidden = jnp.where((line == 0) & (lane >= valid), -1e30, 0.0).astype(BF)
        k3 = jnp.concatenate([keys, keys, keys, hidden, jnp.zeros_like(hidden)], axis=0)
        s = jnp.dot(q3, k3, preferred_element_type=F32)
        e[g, i] = jnp.exp2(s - jnp.max(s, axis=1, keepdims=True))
        for part in range(2):
            lines = qc[g, part, i].T
            for n in range(4):
                qs[n, g, part, i] = lines[n * part_rows : (n + 1) * part_rows].T
        gws[g, i] = jnp.dot(qc[g, 1, i].T, kv[g, 1, i], preferred_element_type=F32)
        return carry

    def early_rows(g):
        lax.fori_loop(g * rows_dev, (g + 1) * rows_dev, early, 0)

    early_rows(core)
    take(mswap[1], rd)
    take(mlen[1], lens.at[0])
    early_rows(1 - core)
    acc[...] = jnp.zeros_like(acc)
    total[...] = jnp.zeros_like(total)

    def chunks(n):
        if n < 2:
            return nz // 2, NY, lambda zz: (0, n * nz // 2 + zz, slice(None))
        return nz, NY // 2, lambda zz: (1, zz, slice((n - 2) * NY // 2, (n - 1) * NY // 2))

    def lay(n):
        count, wide, at = chunks(n)

        def part(zz, carry):
            stage[: wide * NC * 16] = (
                bg[at(zz)].astype(F32).reshape(wide * NC * 16, 128) * LOG2E
            )
            for g in range(wide * NC // 4):
                for t in range(8):
                    j0 = pl.multiple_of(n * part_rows + zz * (wide * NC * 2) + g * 8, 8)
                    eb[pl.ds(j0, 8), t * 128 : (t + 1) * 128] = jnp.exp2(
                        stage[pl.ds(g * 64 + t, 8, stride=8), :]
                    )
            return carry

        lax.fori_loop(0, count, part, 0)

    def late(n, g):
        rows = slice(n * part_rows, (n + 1) * part_rows)

        def one(i, carry):
            p = e[g, i, rows] * eb[rows]
            gw = gws[g, i, rows]
            inv = 1.0 / jnp.sum(p, axis=1, keepdims=True)
            w = p * inv
            grad = w * (gw - jnp.sum(p * gw, axis=1, keepdims=True) * inv)
            total[rows] += grad
            low = grad.astype(BF)
            gqs[n, g, i] = lax.dot_general(
                kv[g, 0, i], low, (((1,), (1,)), ((), ())), preferred_element_type=F32
            )
            acc[g, 0, i] += jnp.dot(qs[n, g, 0, i], low, preferred_element_type=F32)
            acc[g, 1, i] += jnp.dot(qs[n, g, 1, i], w.astype(BF), preferred_element_type=F32)
            return carry

        lax.fori_loop(0, rows_dev, one, 0, unroll=4)

    def unlay(n):
        count, wide, at = chunks(n)

        def part(zz, carry):
            for g in range(wide * NC // 4):
                for t in range(8):
                    j0 = pl.multiple_of(n * part_rows + zz * (wide * NC * 2) + g * 8, 8)
                    stage[pl.ds(g * 64 + t, 8, stride=8), :] = total[
                        pl.ds(j0, 8), t * 128 : (t + 1) * 128
                    ]
            gbs[at(zz)] = stage[: wide * NC * 16].reshape(wide, NC, 16, 128).astype(BF)
            return carry

        lax.fori_loop(0, count, part, 0)

    order = (0, 2, 3, 1)
    sum2 = {}
    for turn, n in enumerate(order):
        take(m2[n][1], r2a.at[0] if n < 2 else r2b.at[0])
        lay(n)
        late(n, 1 - core)
        if turn == 3:
            for i in range(rows_dev):
                dkv[1 - core, 0, i] = (acc[1 - core, 0, i] * factor).astype(BF)
                dkv[1 - core, 1, i] = acc[1 - core, 1, i].astype(BF)
            give = start([remote(dkv.at[1 - core], rd, nswap, (other, key))])
        late(n, core)
        unlay(n)
        if n < 2:
            sum2[n] = [
                remote(
                    gbs.at[0, n * nz // 2 : (n + 1) * nz // 2, lax.rem(y + s, NY)],
                    r2a.at[n, s - 1], n2[n], y_peer(s),
                )
                for s in ys
            ]
        else:
            sum2[n] = [
                remote(
                    gbs.at[1, lax.rem(z + s, nz), (n - 2) * NY // 2 : (n - 1) * NY // 2],
                    r2b.at[n - 2, s - 1], n2[n], z_peer(s),
                )
                for s in zs
            ]
        start(sum2[n])
    for g in range(NC):
        for i in range(rows_dev):
            gq[g, i] = (
                jnp.concatenate([gqs[n, g, i] for n in range(4)], axis=1) * factor
            ).astype(BF)

    backs = []
    for b in range(2):
        for g in range(NC):
            away = jnp.logical_not((x == core * 2 + b) & (core == g))
            piece = gq.at[g, :, :, b * 128 : (b + 1) * 128]
            owner = (row_of(z, y, g), a * NX + core * 2 + b)
            cp = remote(piece, rq.at[x], ngq, owner)
            pl.when(away)(cp.start)
            keep = pltpu.make_async_copy(piece, rq.at[x], loc.at[2])
            pl.when(jnp.logical_not(away))(keep.start)
            backs.append((away, keep))
    take(nswap[1], rd)
    for i in range(rows_dev):
        sd[0, i] = (acc[core, 0, i] * factor + rd[0, i].astype(F32)).astype(BF)
        sd[1, i] = (acc[core, 1, i] + rd[1, i].astype(F32)).astype(BF)
    outs = []
    for s in (6, 2, 5, 7, 1, 3, 4):
        to = lax.rem(key + s, NA * NX)
        outs.append(
            remote(
                sd.at[:, :, :, pl.ds(to * 128, 128)], rk.at[key], nkv, (row, to)
            )
        )
    start(outs)
    held = start(
        [pltpu.make_async_copy(sd.at[:, :, :, pl.ds(key * 128, 128)], rk.at[key], loc.at[3])]
    )

    take(n2[2][1], r2b.at[0])
    take(n2[3][1], r2b.at[1])
    for n in range(2):
        part = gbs[1, z, n * NY // 2 : (n + 1) * NY // 2].astype(F32)
        for s in range(nz - 1):
            part += r2b[n, s].astype(F32)
        s2b[n * NY // 2 : (n + 1) * NY // 2] = part.astype(BF)
    def home(even, source):
        for maybe, same, zy, g, peer in owners(even):
            cp = remote(source.at[zy, g], r5.at[x * NY + (z if even else y)], n4, peer)
            if maybe:
                pl.when(jnp.logical_not(same))(cp.start)
            else:
                cp.start()

    home(False, s2b)
    take(n2[0][1], r2a.at[0])
    take(n2[1][1], r2a.at[1])
    for n in range(2):
        part = gbs[0, n * nz // 2 : (n + 1) * nz // 2, y].astype(F32)
        for s in range(NY - 1):
            part += r2a[n, s].astype(F32)
        s2a[n * nz // 2 : (n + 1) * nz // 2] = part.astype(BF)
    home(True, s2a)
    pl.when(here & (side == 0))(lambda: r5.__setitem__(x * NY + z, s2a[z, core]))
    pl.when(here & (side == 1))(lambda: r5.__setitem__(x * NY + y, s2b[y, core]))
    take(nkv[1], rk.at[0:7])
    held[0].wait()
    for i in range(rows_dev):
        for part in range(2):
            both = [
                rk[h, part, i].astype(F32) + rk[NX + h, part, i].astype(F32) for h in range(NX)
            ]
            done[1 + part, i] = jnp.concatenate(both, axis=0).astype(BF).T
    leaving = start([pltpu.make_async_copy(done.at[1], ok, loc.at[8]), pltpu.make_async_copy(done.at[2], ov, loc.at[9])])
    for away, keep in backs:
        pl.when(jnp.logical_not(away))(keep.wait)
    take_some(ngq[1], rq)
    for i in range(rows_dev):
        turned = jnp.concatenate([rq[h, i] for h in range(NX)], axis=0).T
        for n in range(2 * nz):
            at = jnp.where(side == 1, (n % nz) * 2 + n // nz, n)
            done[0, i, pl.ds(pl.multiple_of(at * 16, 16), 16)] = turned[n * 16 : (n + 1) * 16]
    leaving += start([pltpu.make_async_copy(done.at[0], oq, loc.at[10])])
    for even, count in ((True, nz), (False, NY)):

        @pl.when(side == (0 if even else 1))
        def _():
            pl.when(here)(lambda: take(n4[1], r5.at[0 : NX * count - 1]))
            pl.when(jnp.logical_not(here))(lambda: take(n4[1], r5.at[0 : NX * count]))
            for h in range(NX):
                part = r5[h * NY].astype(F32)
                for n in range(1, count):
                    part += r5[h * NY + n].astype(F32)
                r4[h] = part

    take_some(m0[0], pieces)
    take_some(mqc[0], qcs)
    take_some(ngq[0], rq)
    pl.when(here)(lambda: take(n4[0], r5.at[0:23]))
    pl.when(jnp.logical_not(here))(lambda: take(n4[0], r5.at[0:24]))
    for group, like in (
        (m1a, r3a), (m1b, r3b), (mkv, rk.at[0:7]), (nkv, rk.at[0:7]),
        (mswap, rd), (nswap, rd), (mlen, lens.at[0]),
    ):
        take(group[0], like)
    for group in (m2, n2):
        for n in range(4):
            take(group[n][0], r2a.at[0] if n < 2 else r2b.at[0])
    for cp in leaving:
        cp.wait()


def finish(q_in, k_in, v_in, r4, oq, ok, ov, ob):
    oq[...] = q_in[...]
    ok[...] = k_in[...]
    ov[...] = v_in[...]
    for h in range(NX):
        for j in range(2):
            for t in range(8):
                n = j * 8 + t
                ob[h, j : j + 1, t * 128 : (t + 1) * 128] = r4[h, n : n + 1, :]


def dma(*shape):
    return pltpu.SemaphoreType.DMA(shape)


def per_device(queries, keys_in, values, cotangent, pair_bias, key_lengths):
    rows_dev, block, feature = queries.shape
    heads, owned, length = pair_bias.shape
    dim = feature // heads
    nz = lax.axis_size("row") // (NY * NC)
    tile = (owned * length // 128, 128)
    span = 2 * block
    vmem = pl.BlockSpec(memory_space=VM)
    kind = jax.ShapeDtypeStruct(queries.shape, BF)
    scratch = [
        VM(queries.shape, BF),
        VM(queries.shape, BF),
        VM(queries.shape, BF),
        VM(queries.shape, BF),
        VM((NX, rows_dev, dim, block), BF),
        VM((3,) + queries.shape, BF),
        VM((NX,) + tile, BF),
        VM((2, NC) + tile, BF),
        VM((2, nz, NY, NC) + tile, BF),
        VM((NX, 2, rows_dev, dim, block), BF),
        VM((NX, 2, rows_dev, dim, block), BF),
        VM((NC, 2, rows_dev, dim, length), BF),
        VM((NC, 2, rows_dev, dim, span), BF),
        VM((4, NC, 2, rows_dev, dim, span // 4), BF),
        VM((NC, 8, 128), F32),
        VM((NY * NC * tile[0], 128), F32),
        VM((span, length), F32),
        VM((NC, rows_dev, span, length), F32),
        VM((NC, rows_dev, span, length), F32),
        VM((span, length), F32),
        VM((NC, 2, rows_dev, dim, length), F32),
        VM((NC, 2, rows_dev, dim, length), BF),
        VM((4, NC, rows_dev, dim, span // 4), F32),
        VM((NC, rows_dev, dim, span), BF),
        VM((2, rows_dev, dim, length), BF),
        VM((2, rows_dev, dim, length), BF),
        VM((2, nz, NY, NC) + tile, BF),
        VM((2, NY - 1, nz // 2, NC) + tile, BF),
        VM((2, nz - 1, NY // 2, NC) + tile, BF),
        VM((nz, NC) + tile, BF),
        VM((NY, NC) + tile, BF),
        VM((nz - 1, NC) + tile, BF),
        VM((NY - 1, NC) + tile, BF),
        VM((NX * NY,) + tile, BF),
        VM((NA * NX, 2, rows_dev, dim, block), BF),
        dma(11),
        dma(EXCHANGES),
        dma(EXCHANGES),
    ]
    passed = (kind, kind, kind, jax.ShapeDtypeStruct((heads,) + tile, F32))
    away = pl.BlockSpec(memory_space=pl.ANY)
    parts = pl.pallas_call(
        lambda *refs: kernel(nz, *refs),
        out_shape=passed,
        in_specs=[pl.BlockSpec(memory_space=pltpu.SMEM)] + [away] * 4 + [vmem],
        out_specs=(away,) * 3 + (vmem,),
        scratch_shapes=scratch,
        compiler_params=pltpu.CompilerParams(
            collective_id=0, has_side_effects=True, vmem_limit_bytes=60 * 1024 * 1024
        ),
        name="attention_grad",
    )(key_lengths, queries, keys_in, values, cotangent, pair_bias)
    return pl.pallas_call(
        finish,
        out_shape=(kind, kind, kind, jax.ShapeDtypeStruct(pair_bias.shape, F32)),
        in_specs=[vmem] * 4,
        out_specs=(vmem,) * 4,
        compiler_params=pltpu.CompilerParams(vmem_limit_bytes=60 * 1024 * 1024),
        name="finish",
    )(*parts)


def solution(mesh):
    wide = P("row", "key", None)
    bias = P(None, ("key", "row"), None)
    return jax.shard_map(
        per_device,
        mesh=mesh,
        in_specs=(wide, wide, wide, wide, bias, P("row")),
        out_specs=(wide, wide, wide, bias),
        check_vma=False,
    )
```
